32 devices in a mesh: seq: 8 (over z, x), dp: 4 (over y, core).
Axes of the slice: x: 2, y: 2, z: 4, core: 2. Of those that a mesh axis runs over, the one named last changes fastest.
Arguments:
- x_in: bfloat16 [4, 2048, 2048], P('dp', 'seq'), may hold values from -6 to 6
- gate_in: bfloat16 [4, 2048, 2048], P('dp', 'seq'), may hold values from -6 to 6
- keys_b: bfloat16 [4, 2048, 128], P('dp', 'seq'), may hold values from -6 to 6
- queries_c: bfloat16 [4, 2048, 128], P('dp', 'seq'), may hold values from -0.5 to 0.5
- decay_log: float32 [4, 32, 2048], P('dp', None, 'seq'), may hold values from -0.8 to 0
- level_mix: float32 [4, 12, 32, 2048], P('dp', None, None, 'seq'), may hold values from 0.2 to 2
- norm_gain: float32 [2048], replicated, may hold values from 0.25 to 1.75
- w_gate: bfloat16 [2048, 2816], P(None, ('seq', 'dp')), may hold values from -0.125 to 0.125
- w_up: bfloat16 [2048, 2816], P(None, ('seq', 'dp')), may hold values from -0.125 to 0.125
Outputs:
- hidden: bfloat16 [4, 2048, 2816], P('dp', 'seq')
The draws below stay inside these ranges and needn't reach their ends.
All inputs are finite; a program needn't handle non-finite values.
Results may differ from the reference program's by a relative error of at most 0.0078.
Values may be sent and summed in bfloat16 or wider, within the bound.
A program may use at most 128 MiB of HBM per device.

```python
import math
import jax
import jax.numpy as jnp
from jax import lax

HEADS = 32
HEAD_DIM = 64
STATE = 128
FF = 2816
SPAN = 256
SPAN_BITS = 8
D = 2048
TOK_DEV = 256
SEQUENCE_TOKENS = 2048
SEQUENCE_COUNT = 4
FENWICK_LEVELS = 12


def draw_decay_log(key, part):
    key = jax.random.fold_in(key, 11)
    k_fast, k_slow, k_quick, k_dev, k_tok, key_position, k_loss = jax.random.split(key, 7)
    devices = SEQUENCE_TOKENS // TOK_DEV
    fast = jax.random.uniform(k_fast, (SEQUENCE_COUNT, HEADS, 1)) < 0.5
    tok_scale = jnp.exp(jax.random.uniform(k_tok, (SEQUENCE_COUNT, HEADS, SEQUENCE_TOKENS), minval=math.log(0.5), maxval=math.log(1.5)))
    slow_rate = jax.random.uniform(k_slow, (SEQUENCE_COUNT, HEADS, 1), minval=0.1, maxval=0.35) / SEQUENCE_TOKENS
    quick_rate = jnp.exp(jax.random.uniform(k_quick, (SEQUENCE_COUNT, HEADS, 1), minval=math.log(1.0 / 50.0), maxval=math.log(1.0 / 30.0)))
    base_rate = jnp.where(fast, quick_rate, slow_rate)
    dev_scale = jnp.exp(jax.random.uniform(k_dev, (SEQUENCE_COUNT, HEADS, devices), minval=math.log(0.5), maxval=math.log(1.5)))
    dev_scale = jnp.repeat(dev_scale, TOK_DEV, axis=2)
    surge_position = jax.random.randint(key_position, (SEQUENCE_COUNT, 1, 1, 2), 0, SEQUENCE_TOKENS)
    level_match = jnp.any(jnp.arange(SEQUENCE_TOKENS)[None, None, :, None] == surge_position, axis=-1)
    loss = jax.random.uniform(k_loss, (SEQUENCE_COUNT, HEADS, SEQUENCE_TOKENS), minval=0.22, maxval=0.69)
    return -(base_rate * dev_scale * tok_scale) - jnp.where(level_match, loss, 0.0)


def shard_levels(own_key, extent, cuts, least, largest):
    gain, own = 1.0, jax.random.fold_in(own_key, 6)
    for dim, blocks in cuts:
        draws = jnp.exp(jax.random.uniform(jax.random.fold_in(own, dim), (blocks,), jnp.float32, least / len(cuts), largest / len(cuts)))
        gain = gain * jnp.repeat(draws, extent[dim] // blocks).reshape([-1 if axis == dim else 1 for axis in range(len(extent))])
    return gain


def bell_draw(own_key, dims, deviation, most, shards=(), kind=jnp.bfloat16):
    array = deviation * jax.random.normal(own_key, dims, jnp.float32)
    if shards:
        array = array * shard_levels(own_key, dims, shards, -0.22, 0.18)
    return jnp.clip(array, -most, most).astype(kind)


def setup_inputs(seed: int = 0) -> dict:
    arg_keys = jax.random.split(jax.random.key(seed), 10)
    x_in = bell_draw(arg_keys[0], (SEQUENCE_COUNT, SEQUENCE_TOKENS, D), 1.0, 6.0, ((0, 4), (1, 8)))
    gate_in = bell_draw(arg_keys[1], (SEQUENCE_COUNT, SEQUENCE_TOKENS, D), 1.0, 6.0, ((0, 4), (1, 8)))
    keys_b = bell_draw(arg_keys[2], (SEQUENCE_COUNT, SEQUENCE_TOKENS, STATE), 1.0, 6.0, ((0, 4), (1, 8)))
    queries_c = bell_draw(arg_keys[3], (SEQUENCE_COUNT, SEQUENCE_TOKENS, STATE), STATE ** -0.5, 0.5, ((0, 4), (1, 8)))
    decay_log = draw_decay_log(jax.random.fold_in(arg_keys[9], 71), 0)
    level_mix = jnp.clip(jnp.exp(math.log(2.0) - 2.3025851 * jax.random.uniform(arg_keys[5], (SEQUENCE_COUNT, FENWICK_LEVELS, HEADS, SEQUENCE_TOKENS), jnp.float32) ** shard_levels(arg_keys[5], (SEQUENCE_COUNT, FENWICK_LEVELS, HEADS, SEQUENCE_TOKENS), ((0, 4), (3, 8)), -0.2, 0.2)), 0.2, 2.0)
    norm_gain = jnp.clip(1.0 + 0.15 * jax.random.normal(arg_keys[6], (D,), jnp.float32), 0.25, 1.75)
    w_gate = bell_draw(arg_keys[7], (D, FF), D ** -0.5, 0.125, ((1, 32),))
    w_up = bell_draw(arg_keys[8], (D, FF), D ** -0.5, 0.125, ((1, 32),))
    return {"x_in": x_in, "gate_in": gate_in, "keys_b": keys_b, "queries_c": queries_c, "decay_log": decay_log, "level_mix": level_mix, "norm_gain": norm_gain, "w_gate": w_gate, "w_up": w_up}


EPS = 1e-05
HIGH = lax.Precision.HIGHEST

def top_bit(values):
    powers = jnp.arange(1, 31, dtype=jnp.int32)
    return lax.optimization_barrier(jnp.sum(values[..., None] >> powers > 0, axis=-1)).astype(jnp.int32)

def rounded(values):
    return lax.optimization_barrier(values.astype(jnp.bfloat16)).astype(jnp.float32)

def block_inner(x_blk, b_blk, c_blk, a_blk, mix_low):
    length = a_blk.shape[1]
    inner_count = mix_low.shape[0]
    running = jnp.cumsum(a_blk, axis=1)
    position = jnp.arange(length, dtype=jnp.int32)
    differ = position[:, None] ^ position[None, :]
    level_table = jnp.where(differ > 0, top_bit(differ) + 1, 0)
    level_picks = (level_table[None] == jnp.arange(inner_count, dtype=jnp.int32)[:, None, None]).astype(jnp.float32)
    chosen = jnp.einsum('lht,lts->hts', mix_low, level_picks, precision=HIGH)
    causal_mask = position[:, None] >= position[None, :]
    log_gap = jnp.where(causal_mask[None], running[:, :, None] - running[:, None, :], -jnp.inf)
    scores = jnp.dot(c_blk, b_blk.T, preferred_element_type=jnp.float32)
    weights = rounded(chosen * jnp.exp(log_gap) * scores[None])
    local_part = jnp.einsum('hts,shp->thp', weights, x_blk.astype(jnp.float32), precision=HIGH)
    tail_decay = jnp.exp(running[:, -1:] - running)
    scaled_keys = rounded(tail_decay.T[:, :, None] * b_blk[:, None, :].astype(jnp.float32))
    block_state = jnp.einsum('shn,shp->hnp', scaled_keys, x_blk.astype(jnp.float32), precision=HIGH)
    return (local_part, block_state, running)

def block_distant(c_blk, running, mix_high, levels):
    growth = jnp.exp(running)
    distant_sum = jnp.zeros((c_blk.shape[0], running.shape[0], levels[0].shape[2]), jnp.float32)
    for level_rank in range(len(levels)):
        level_scale = (mix_high[level_rank] * growth).T
        product = jnp.einsum('tn,hnp->thp', c_blk.astype(jnp.float32), rounded(levels[level_rank]), precision=HIGH)
        distant_sum = distant_sum + level_scale[:, :, None] * product
    return distant_sum

def reference(x_in, gate_in, keys_b, queries_c, decay_log, level_mix, norm_gain, w_gate, w_up):
    span_count = SEQUENCE_TOKENS // SPAN
    inner_count = SPAN_BITS + 1
    outer_count = FENWICK_LEVELS - inner_count

    def per_sequence(items):
        x_seq, z_seq, b_seq, c_seq, a_seq, mix_seq = items
        x_blocks = x_seq.reshape(span_count, SPAN, HEADS, HEAD_DIM)
        b_blocks = b_seq.reshape(span_count, SPAN, STATE)
        c_blocks = c_seq.reshape(span_count, SPAN, STATE)
        a_blocks = a_seq.reshape(HEADS, span_count, SPAN).transpose(1, 0, 2)
        mix_blocks = mix_seq.reshape(FENWICK_LEVELS, HEADS, span_count, SPAN).transpose(2, 0, 1, 3)

        def first_pass(block_items):
            x_blk, b_blk, c_blk, a_blk, mix_blk = block_items
            return block_inner(x_blk, b_blk, c_blk, a_blk, mix_blk[:inner_count])
        local_parts, block_states, runnings = lax.map(first_pass, (x_blocks, b_blocks, c_blocks, a_blocks, mix_blocks))
        block_decays = runnings[:, :, -1]
        before = jnp.concatenate([jnp.zeros((1, HEADS), jnp.float32), jnp.cumsum(block_decays, axis=0)], axis=0)
        span_ids = jnp.arange(span_count, dtype=jnp.int32)

        def second_pass(block_items):
            here, c_blk, running, mix_blk = block_items
            level_ids = inner_count + top_bit(here ^ span_ids)
            earlier = span_ids < here
            log_gap = before[here][None, :] - before[1:]
            levels = []
            for level_rank in range(outer_count):
                keep = earlier & (level_ids == inner_count + level_rank)
                factor = jnp.exp(jnp.where(keep[:, None], log_gap, -jnp.inf))
                levels.append(jnp.einsum('ih,ihnp->hnp', factor, block_states, precision=HIGH))
            return block_distant(c_blk, running, mix_blk[inner_count:], levels)
        distant = lax.map(second_pass, (span_ids, c_blocks, runnings, mix_blocks))
        mixed = (local_parts + distant).reshape(SEQUENCE_TOKENS, HEADS * HEAD_DIM)
        gated = mixed * jax.nn.silu(z_seq.astype(jnp.float32))
        normed = (gated * lax.rsqrt(lax.optimization_barrier(jnp.mean(gated * gated, axis=-1, keepdims=True)) + EPS) * norm_gain).astype(jnp.bfloat16)
        gate_pre = jnp.dot(normed, w_gate, preferred_element_type=jnp.float32)
        up_pre = jnp.dot(normed, w_up, preferred_element_type=jnp.float32)
        return (jax.nn.silu(gate_pre) * up_pre).astype(jnp.bfloat16)
    return lax.map(per_sequence, (x_in, gate_in, keys_b, queries_c, decay_log, level_mix))
```

```python
import jax
import jax.numpy as jnp
from jax import lax
from jax.experimental import pallas as pl
from jax.experimental.pallas import tpu as pltpu
from jax.sharding import PartitionSpec as P

SPAN = 256
SPAN_BITS = 8


EPS = 1e-05
HIGH = lax.Precision.HIGHEST


def swapped(value, axis, distance):
    mask = 2**distance
    pairs = [(source, source ^ mask) for source in range(lax.axis_size(axis))]
    return lax.ppermute(value, axis, pairs)


def top_bit(values):
    powers = jnp.arange(1, 31, dtype=jnp.int32)
    return jnp.sum(values[..., None] >> powers > 0, axis=-1)


def block_inner(x_blk, b_blk, c_blk, a_blk, mix_low):
    length = a_blk.shape[1]
    inner_count = mix_low.shape[0]
    running = jnp.cumsum(a_blk, axis=1)
    position = jnp.arange(length, dtype=jnp.int32)
    differ = position[:, None] ^ position[None, :]
    level_table = jnp.where(differ > 0, top_bit(differ) + 1, 0)
    level_picks = (
        level_table[None] == jnp.arange(inner_count, dtype=jnp.int32)[:, None, None]
    ).astype(jnp.float32)
    chosen = jnp.einsum("lht,lts->hts", mix_low, level_picks, precision=HIGH)
    causal_mask = position[:, None] >= position[None, :]
    log_gap = jnp.where(causal_mask[None], running[:, :, None] - running[:, None, :], -jnp.inf)
    scores = jnp.dot(c_blk, b_blk.T, preferred_element_type=jnp.float32)
    weights = (chosen * jnp.exp(log_gap) * scores[None]).astype(jnp.bfloat16)
    local_part = jnp.einsum("hts,shp->thp", weights, x_blk, preferred_element_type=jnp.float32)
    tail_decay = jnp.exp(running[:, -1:] - running)
    scaled_keys = (tail_decay.T[:, :, None] * b_blk[:, None, :]).astype(jnp.bfloat16)
    block_state = jnp.einsum("shn,shp->hnp", scaled_keys, x_blk, preferred_element_type=jnp.float32)
    return (local_part, block_state, running)


def block_distant(c_blk, running, mix_high, levels):
    growth = jnp.exp(running)
    distant_sum = jnp.zeros((c_blk.shape[0], running.shape[0], levels[0].shape[2]), jnp.float32)
    for level_rank in range(len(levels)):
        level_scale = (mix_high[level_rank] * growth).T
        product = jnp.einsum(
            "tn,hnp->thp",
            c_blk,
            levels[level_rank].astype(jnp.bfloat16),
            preferred_element_type=jnp.float32,
        )
        distant_sum = distant_sum + level_scale[:, :, None] * product
    return distant_sum


def gathered_projection(normed, w_gate, w_up):
    tok_dev = normed.shape[0]
    paired = jnp.stack([w_gate, w_up])
    dp_count = lax.axis_size("dp")
    seq_count = lax.axis_size("seq")
    seq_weights = lax.all_gather(paired, "seq", axis=2, tiled=True)
    projected = jnp.einsum(
        "td,gdk->gtk",
        normed,
        lax.all_gather(seq_weights, "dp", axis=2, tiled=True),
        preferred_element_type=jnp.float32,
    )
    returned = (jax.nn.silu(projected[0]) * projected[1]).astype(jnp.bfloat16)
    hidden = (
        returned.reshape(tok_dev, dp_count, seq_count, -1)
        .transpose(0, 2, 1, 3)
        .reshape(tok_dev, -1)
    )
    return hidden


MESH = pl.DeviceIdType.MESH
SEQ_COUNT = 8
DP_COUNT = 4
LINE = 4
CHIPS = 16


def line_member(z, steps):
    place = z + (z >= 2) * (5 - 2 * z)
    back = lax.rem(place - steps + 2 * LINE, LINE)
    return back + (back >= 2) * (5 - 2 * back)


class Gather:
    def __init__(self, piece, held, z_sems, x_sems, y_sems, core_sems, own_sem):
        self.piece, self.held, self.own_sem = piece, held, own_sem
        self.sems = {"z": z_sems, "x": x_sems, "y": y_sems, "core": core_sems}
        seq, dp = lax.axis_index("seq"), lax.axis_index("dp")
        self.z, self.x, self.y, self.core = seq // 2, lax.rem(seq, 2), dp // 2, lax.rem(dp, 2)
        self.targets = {
            "z": (line_member(self.z, -1) * 2 + self.x, dp),
            "x": (self.z * 2 + 1 - self.x, dp),
            "y": (seq, (1 - self.y) * 2 + self.core),
            "core": (seq, self.y * 2 + 1 - self.core),
        }
        self.before = (line_member(self.z, 1) * 2 + self.x, dp)
        self.sent = []

    def greet(self):
        barrier = pltpu.get_barrier_semaphore()
        others = list(self.targets.values()) + [self.before]
        for other in others:
            pl.semaphore_signal(barrier, inc=1, device_id=other, device_id_type=MESH)
        pl.semaphore_wait(barrier, len(others))

    def chip(self, step, flip_x, flip_y):
        x = 1 - self.x if flip_x else self.x
        y = 1 - self.y if flip_y else self.y
        return line_member(self.z, step) * 4 + x * 2 + y

    def copy(self, way, slot, chip, own=False):
        place = self.held.at[self.core, chip]
        return pltpu.make_async_remote_copy(
            src_ref=self.piece if own else place,
            dst_ref=place,
            send_sem=self.sems[way].at[0, slot],
            recv_sem=self.sems[way].at[1, slot],
            device_id=self.targets[way],
            device_id_type=MESH,
        )

    def send(self, way, slot, chip, own=False):
        copy = self.copy(way, slot, chip, own)
        copy.start()
        self.sent.append(copy)

    def start(self):
        chip = self.chip(0, 0, 0)
        self.own = pltpu.make_async_copy(self.piece, self.held.at[self.core, chip], self.own_sem)
        self.own.start()
        for way in ("z", "x", "y", "core"):
            self.send(way, 0, chip, own=True)

    def line(self, step):
        chip = self.chip(step, 0, 0)
        self.copy("z", step - 1, chip).wait_recv()
        if step < LINE - 1:
            self.send("z", step, chip)
        for way in ("x", "y"):
            self.send(way, step, chip)
        self.send("core", step * 4, chip)

    def across_x(self, step):
        chip = self.chip(step, 1, 0)
        self.copy("x", step, chip).wait_recv()
        if step < 2:
            self.send("y", LINE + step, chip)
        self.send("core", step * 4 + 1, chip)

    def across_y(self, step):
        chip = self.chip(step, 0, 1)
        self.copy("y", step, chip).wait_recv()
        if step >= 2:
            self.send("x", LINE + step - 2, chip)
        self.send("core", step * 4 + 2, chip)

    def corner(self, step):
        chip = self.chip(step, 1, 1)
        way = "y" if step < 2 else "x"
        self.copy(way, LINE + step % 2, chip).wait_recv()
        self.send("core", step * 4 + 3, chip)

    def ready(self, step, kind):
        chip = self.chip(step, kind % 2, kind // 2)
        place = self.held.at[1 - self.core, chip]
        pltpu.make_async_remote_copy(
            src_ref=place,
            dst_ref=place,
            send_sem=self.sems["core"].at[0, step * 4 + kind],
            recv_sem=self.sems["core"].at[1, step * 4 + kind],
            device_id=self.targets["core"],
            device_id_type=MESH,
        ).wait_recv()
        return chip

    def finish(self):
        for copy in self.sent:
            copy.wait_send()


def project(normed, held, hidden, chip):
    contract = (((1,), (1,)), ((), ()))
    gate = lax.dot_general(normed[...], held[0, chip], contract, preferred_element_type=jnp.float32)
    up = lax.dot_general(normed[...], held[1, chip], contract, preferred_element_type=jnp.float32)
    hidden[chip] = (gate / (1.0 + jnp.exp(-gate)) * up).astype(hidden.dtype)


def projection_kernel(normed, piece, hidden, held, z_sems, x_sems, y_sems, core_sems, own_sem):
    gather = Gather(piece, held, z_sems, x_sems, y_sems, core_sems, own_sem)
    gather.greet()
    gather.start()
    gather.own.wait()
    project(normed, held, hidden, gather.ready(0, 0))
    for step in range(LINE):
        gather.across_x(step)
        gather.across_y(step)
        if step + 1 < LINE:
            gather.line(step + 1)
        project(normed, held, hidden, gather.ready(step, 1))
        project(normed, held, hidden, gather.ready(step, 2))
        if step >= 1:
            gather.corner(step - 1)
            project(normed, held, hidden, gather.ready(step - 1, 3))
        if step + 1 < LINE:
            project(normed, held, hidden, gather.ready(step + 1, 0))
    gather.corner(LINE - 1)
    project(normed, held, hidden, gather.ready(LINE - 1, 3))
    gather.finish()


def chip_rows(w_gate, w_up):
    first = lax.axis_index("dp") % 2 == 0
    gate, up = w_gate.T, w_up.T
    pairs = [(source, source ^ 1) for source in range(DP_COUNT)]
    other = lax.ppermute(jnp.where(first, up, gate), "dp", pairs)
    return jnp.where(first, jnp.concatenate([gate, other]), jnp.concatenate([other, up]))


def streamed_projection(normed, w_gate, w_up):
    piece = chip_rows(w_gate, w_up)
    rows, depth = piece.shape
    tokens = normed.shape[0]
    sems = pltpu.SemaphoreType.DMA
    hidden = pl.pallas_call(
        projection_kernel,
        out_shape=jax.ShapeDtypeStruct((CHIPS, tokens, rows), jnp.bfloat16),
        in_specs=[pl.BlockSpec(memory_space=pltpu.VMEM)] * 2,
        out_specs=pl.BlockSpec(memory_space=pltpu.VMEM),
        scratch_shapes=[
            pltpu.VMEM((2, CHIPS, rows, depth), jnp.bfloat16),
            sems((2, 3)),
            sems((2, 6)),
            sems((2, 6)),
            sems((2, CHIPS)),
            sems,
        ],
        compiler_params=pltpu.CompilerParams(
            collective_id=0, has_side_effects=True, vmem_limit_bytes=48 * 2**20
        ),
        cost_estimate=pl.CostEstimate(
            flops=4 * tokens * CHIPS * rows * depth,
            bytes_accessed=2 * CHIPS * rows * depth * 2,
            transcendentals=tokens * CHIPS * rows,
        ),
    )(normed, piece)
    return hidden.transpose(1, 0, 2).reshape(tokens, CHIPS * rows)


def per_device(x_in, gate_in, keys_b, queries_c, decay_log, level_mix, norm_gain, w_gate, w_up):
    tok_dev = x_in.shape[1]
    embedding_width = x_in.shape[2]
    head_count = decay_log.shape[1]
    head_dim = embedding_width // head_count
    blocks = tok_dev // SPAN
    inner_count = SPAN_BITS + 1
    seq_bits = lax.axis_size("seq").bit_length() - 1
    x_blocks = x_in[0].reshape(blocks, SPAN, head_count, head_dim)
    b_blocks = keys_b[0].reshape(blocks, SPAN, -1)
    c_blocks = queries_c[0].reshape(blocks, SPAN, -1)
    a_blocks = decay_log[0].reshape(head_count, blocks, SPAN)
    mix_all = level_mix[0].reshape(level_mix.shape[1], head_count, blocks, SPAN)
    local_parts, block_states, block_decays, runnings = ([], [], [], [])
    block_index = 0
    local_part, block_state, running = block_inner(
        x_blocks[block_index],
        b_blocks[block_index],
        c_blocks[block_index],
        a_blocks[:, block_index],
        mix_all[:inner_count, :, block_index],
    )
    local_parts.append(local_part)
    block_states.append(block_state)
    block_decays.append(running[:, -1])
    runnings.append(running)
    summary = jnp.zeros_like(block_states[0])
    block_index = 0
    summary = (
        jnp.exp(block_decays[block_index])[:, None, None] * summary + block_states[block_index]
    )
    summary_decay = block_decays[block_index]
    rank_here = lax.axis_index("seq")
    own_prefix = jnp.zeros((head_count,), jnp.float32)
    device_levels = []
    for bit_index in range(seq_bits):
        other_state, other_decay = swapped((summary.astype(jnp.bfloat16), summary_decay), "seq", bit_index)
        other_state = other_state.astype(jnp.float32)
        is_upper = rank_here >> bit_index & 1 == 1
        device_levels.append(
            jnp.where(is_upper, jnp.exp(own_prefix)[:, None, None] * other_state, 0.0)
        )
        lower_state = jnp.where(is_upper, other_state, summary)
        lower_decay = jnp.where(is_upper, other_decay, summary_decay)
        upper_state = jnp.where(is_upper, summary, other_state)
        upper_decay = jnp.where(is_upper, summary_decay, other_decay)
        summary = jnp.exp(upper_decay)[:, None, None] * lower_state + upper_state
        summary_decay = lower_decay + upper_decay
        own_prefix = jnp.where(is_upper, own_prefix + other_decay, own_prefix)
    zero_decay = jnp.zeros((head_count,), jnp.float32)
    block_index = 0
    levels = []
    lead_decay = sum(block_decays[:block_index], zero_decay)
    for device_level in device_levels:
        levels.append(jnp.exp(lead_decay)[:, None, None] * device_level)
    distant = block_distant(
        c_blocks[block_index], runnings[block_index], mix_all[inner_count:, :, block_index], levels
    )
    outputs = local_parts[block_index] + distant
    mixed = outputs.reshape(tok_dev, embedding_width)
    gated = mixed * jax.nn.silu(gate_in[0].astype(jnp.float32))
    normed = (
        gated * lax.rsqrt(jnp.mean(gated * gated, axis=-1, keepdims=True) + EPS) * norm_gain
    ).astype(jnp.bfloat16)
    if (lax.axis_size("seq"), lax.axis_size("dp")) == (SEQ_COUNT, DP_COUNT):
        return streamed_projection(normed, w_gate, w_up)[None]
    return gathered_projection(normed, w_gate, w_up)[None]


def solution(mesh):
    in_specs = (
        P("dp", "seq", None),
        P("dp", "seq", None),
        P("dp", "seq", None),
        P("dp", "seq", None),
        P("dp", None, "seq"),
        P("dp", None, None, "seq"),
        P(),
        P(None, ("seq", "dp")),
        P(None, ("seq", "dp")),
    )
    out_specs = P("dp", "seq", None)
    return jax.shard_map(
        per_device, mesh=mesh, in_specs=in_specs, out_specs=out_specs, check_vma=False
    )
```

```python
import jax
import jax.numpy as jnp
from jax import lax
from jax.experimental import pallas as pl
from jax.experimental.pallas import tpu as pltpu
from jax.sharding import PartitionSpec as P

SPAN = 256
SPAN_BITS = 8


EPS = 1e-05
HIGH = lax.Precision.HIGHEST


def swapped(value, axis, distance):
    mask = 2**distance
    pairs = [(source, source ^ mask) for source in range(lax.axis_size(axis))]
    return lax.ppermute(value, axis, pairs)


def top_bit(values):
    powers = jnp.arange(1, 31, dtype=jnp.int32)
    return jnp.sum(values[..., None] >> powers > 0, axis=-1)


def block_inner(x_blk, b_blk, c_blk, a_blk, mix_low):
    length = a_blk.shape[1]
    inner_count = mix_low.shape[0]
    running = jnp.cumsum(a_blk, axis=1)
    position = jnp.arange(length, dtype=jnp.int32)
    differ = position[:, None] ^ position[None, :]
    level_table = jnp.where(differ > 0, top_bit(differ) + 1, 0)
    level_picks = (
        level_table[None] == jnp.arange(inner_count, dtype=jnp.int32)[:, None, None]
    ).astype(jnp.float32)
    chosen = jnp.einsum("lht,lts->hts", mix_low, level_picks, precision=HIGH)
    causal_mask = position[:, None] >= position[None, :]
    log_gap = jnp.where(causal_mask[None], running[:, :, None] - running[:, None, :], -jnp.inf)
    scores = jnp.dot(c_blk, b_blk.T, preferred_element_type=jnp.float32)
    weights = (chosen * jnp.exp(log_gap) * scores[None]).astype(jnp.bfloat16)
    local_part = jnp.einsum("hts,shp->thp", weights, x_blk, preferred_element_type=jnp.float32)
    tail_decay = jnp.exp(running[:, -1:] - running)
    scaled_keys = (tail_decay.T[:, :, None] * b_blk[:, None, :]).astype(jnp.bfloat16)
    block_state = jnp.einsum("shn,shp->hnp", scaled_keys, x_blk, preferred_element_type=jnp.float32)
    return (local_part, block_state, running)


def block_distant(c_blk, running, mix_high, levels):
    growth = jnp.exp(running)
    distant_sum = jnp.zeros((c_blk.shape[0], running.shape[0], levels[0].shape[2]), jnp.float32)
    for level_rank in range(len(levels)):
        level_scale = (mix_high[level_rank] * growth).T
        product = jnp.einsum(
            "tn,hnp->thp",
            c_blk,
            levels[level_rank].astype(jnp.bfloat16),
            preferred_element_type=jnp.float32,
        )
        distant_sum = distant_sum + level_scale[:, :, None] * product
    return distant_sum


def gathered_projection(normed, w_gate, w_up):
    tok_dev = normed.shape[0]
    paired = jnp.stack([w_gate, w_up])
    dp_count = lax.axis_size("dp")
    seq_count = lax.axis_size("seq")
    seq_weights = lax.all_gather(paired, "seq", axis=2, tiled=True)
    projected = jnp.einsum(
        "td,gdk->gtk",
        normed,
        lax.all_gather(seq_weights, "dp", axis=2, tiled=True),
        preferred_element_type=jnp.float32,
    )
    returned = (jax.nn.silu(projected[0]) * projected[1]).astype(jnp.bfloat16)
    hidden = (
        returned.reshape(tok_dev, dp_count, seq_count, -1)
        .transpose(0, 2, 1, 3)
        .reshape(tok_dev, -1)
    )
    return hidden


MESH = pl.DeviceIdType.MESH
SEQ_COUNT = 8
DP_COUNT = 4
LINE = 4
CHIPS = 16


def line_member(z, steps):
    place = z + (z >= 2) * (5 - 2 * z)
    back = lax.rem(place - steps + 2 * LINE, LINE)
    return back + (back >= 2) * (5 - 2 * back)


class Gather:
    def __init__(self, piece, held, z_sems, x_sems, y_sems, core_sems, own_sem):
        self.piece, self.held, self.own_sem = piece, held, own_sem
        self.sems = {"z": z_sems, "x": x_sems, "y": y_sems, "core": core_sems}
        seq, dp = lax.axis_index("seq"), lax.axis_index("dp")
        self.seq, self.dp = seq, dp
        self.z, self.x, self.y, self.core = seq // 2, lax.rem(seq, 2), dp // 2, lax.rem(dp, 2)
        self.targets = {
            "z": (line_member(self.z, -1) * 2 + self.x, dp),
            "x": (self.z * 2 + 1 - self.x, dp),
            "y": (seq, (1 - self.y) * 2 + self.core),
            "core": (seq, self.y * 2 + 1 - self.core),
        }
        self.before = (line_member(self.z, 1) * 2 + self.x, dp)
        rows = piece.shape[0]
        cut = (rows // 2 + 15) // 16 * 16
        self.cuts = ((0, cut), (cut, rows - cut))
        self.sent = []

    def greet(self):
        barrier = pltpu.get_barrier_semaphore()
        others = list(self.targets.values()) + [self.before]
        for other in others:
            pl.semaphore_signal(barrier, inc=1, device_id=other, device_id_type=MESH)
        pl.semaphore_wait(barrier, len(others))

    def chip(self, step, flip_x, flip_y):
        x = 1 - self.x if flip_x else self.x
        y = 1 - self.y if flip_y else self.y
        return line_member(self.z, step) * 4 + x * 2 + y

    def copy(self, way, slot, chip, part, own=False):
        first, count = self.cuts[part]
        place = self.held.at[self.core, chip, pl.ds(first, count)]
        return pltpu.make_async_remote_copy(
            src_ref=self.piece.at[pl.ds(first, count)] if own else place,
            dst_ref=place,
            send_sem=self.sems[way].at[0, slot],
            recv_sem=self.sems[way].at[1, slot],
            device_id=self.targets[way],
            device_id_type=MESH,
        )

    def send(self, way, slot, chip, part, own=False):
        copy = self.copy(way, slot, chip, part, own)
        copy.start()
        self.sent.append(copy)

    def start(self):
        chip = self.chip(0, 0, 0)
        self.own = pltpu.make_async_copy(self.piece, self.held.at[self.core, chip], self.own_sem)
        self.own.start()
        for way in ("z", "x", "y", "core"):
            for part in range(2):
                self.send(way, part, chip, part, own=True)

    def line(self, step, part):
        chip = self.chip(step, 0, 0)
        self.copy("z", (step - 1) * 2 + part, chip, part).wait_recv()
        if step < LINE - 1:
            self.send("z", step * 2 + part, chip, part)
        for way in ("x", "y"):
            self.send(way, step * 2 + part, chip, part)
        self.send("core", step * 8 + part, chip, part)

    def across_x(self, step, part):
        chip = self.chip(step, 1, 0)
        self.copy("x", step * 2 + part, chip, part).wait_recv()
        if part == 0:
            self.send("y", 2 * LINE + step, chip, part)
        self.send("core", step * 8 + 2 + part, chip, part)

    def across_y(self, step, part):
        chip = self.chip(step, 0, 1)
        self.copy("y", step * 2 + part, chip, part).wait_recv()
        if part == 1:
            self.send("x", 2 * LINE + step, chip, part)
        self.send("core", step * 8 + 4 + part, chip, part)

    def across(self, step, part):
        self.across_x(step, part)
        self.across_y(step, part)

    def corner(self, step):
        chip = self.chip(step, 1, 1)
        for part, way in enumerate(("y", "x")):
            self.copy(way, 2 * LINE + step, chip, part).wait_recv()
            self.send("core", step * 8 + 6 + part, chip, part)

    def ready(self, step, kind):
        chip = self.chip(step, kind % 2, kind // 2)
        for part in range(2):
            first, count = self.cuts[part]
            place = self.held.at[1 - self.core, chip, pl.ds(first, count)]
            slot = step * 8 + kind * 2 + part
            pltpu.make_async_remote_copy(
                src_ref=place,
                dst_ref=place,
                send_sem=self.sems["core"].at[0, slot],
                recv_sem=self.sems["core"].at[1, slot],
                device_id=self.targets["core"],
                device_id_type=MESH,
            ).wait_recv()
        return chip

    def finish(self):
        for copy in self.sent:
            copy.wait_send()


NT = (((1,), (1,)), ((), ()))
HALF = SPAN // 2
GROUP = 4


def rows_of(index, count):
    return pl.ds(pl.multiple_of(index * count, count), count)


def layer_kernel(
    x_in, gate_in, keys, queries, decay, mix, gain, piece, hidden,
    held, x_cols, gate_cols, normed, mixed, run_col, run_row, tail, level_scale,
    level_of, scores, state, state_out, state_in, decay_out, decay_in,
    z_sems, x_sems, y_sems, core_sems, own_sem, state_sems, decay_sems,
):
    gather = Gather(piece, held, z_sems, x_sems, y_sems, core_sems, own_sem)
    gather.greet()
    gather.start()
    heads = decay.shape[0]
    head_dim = x_cols.shape[0] // heads
    seq, dp = gather.seq, gather.dp
    f32, bf16 = jnp.float32, jnp.bfloat16

    def exchange(bit):
        target = (seq + (1 - 2 * (seq // 2**bit % 2)) * 2**bit, dp)
        pairs = [(state_out, state_in, state_sems), (decay_out, decay_in, decay_sems)]
        return [
            pltpu.make_async_remote_copy(
                src_ref=source.at[bit],
                dst_ref=place.at[bit],
                send_sem=sems.at[0, bit],
                recv_sem=sems.at[1, bit],
                device_id=target,
                device_id_type=MESH,
            )
            for source, place, sems in pairs[: 1 if bit == 2 else 2]
        ]

    before = lax.broadcasted_iota(jnp.int32, (SPAN, SPAN), 0)
    after = lax.broadcasted_iota(jnp.int32, (SPAN, SPAN), 1)
    up_to = (before <= after).astype(f32)
    run = jnp.dot(decay[...], up_to, precision=HIGH, preferred_element_type=f32)
    run_row[...] = run
    tail[...] = jnp.exp(jnp.minimum(run[:, SPAN - 1 :] - run, 0.0))
    total = jnp.broadcast_to(run[:, SPAN - 1 :], (heads, 128))
    decay_out[0] = total

    def turn(index, _):
        lanes = rows_of(index, 128)
        x_cols[lanes, :] = x_in[:, lanes].astype(f32).T.astype(bf16)
        return 0

    lax.fori_loop(0, x_cols.shape[0] // 128, turn, 0)

    def block_states(index, _):
        parts = []
        for place in range(GROUP):
            head = index * GROUP + place
            values = x_cols[rows_of(head, head_dim), :].astype(f32) * tail[pl.ds(head, 1), :]
            parts.append(values.astype(bf16))
        rows = rows_of(index, GROUP * head_dim)
        result = jnp.dot(jnp.concatenate(parts), keys[...], preferred_element_type=f32)
        state[rows, :] = result
        state_out[0, rows, :] = result.astype(bf16)
        return 0

    lax.fori_loop(0, heads // GROUP, block_states, 0)
    rounds = [exchange(0)]
    for copy in rounds[0]:
        copy.start()

    gather.line(1, 0)
    gather.across(0, 0)

    columns = lax.dot_general(
        (before >= after).astype(f32), decay[...], NT, precision=HIGH, preferred_element_type=f32
    )
    for head in range(heads):
        run_col[head] = jnp.broadcast_to(columns[:, head : head + 1], (SPAN, 128))
    scores[...] = lax.dot_general(keys[...], queries[...], NT, preferred_element_type=f32)
    source = lax.broadcasted_iota(jnp.int32, (HALF, HALF), 0)
    target = lax.broadcasted_iota(jnp.int32, (HALF, HALF), 1)
    differ = source ^ target
    level = jnp.zeros((HALF, HALF), jnp.int32)
    for bit in range(SPAN_BITS - 1):
        level = level + (differ >= 2**bit).astype(jnp.int32)
    level_of[...] = jnp.where(source <= target, level, -1)

    gather.line(1, 1)
    gather.across(0, 1)

    def local(head, _):
        run_t = run_row[pl.ds(head, 1), :]
        mixes = [mix[rank, pl.ds(head, 1), :] for rank in range(SPAN_BITS + 1)]
        values = x_cols[rows_of(head, head_dim), :]
        weights = []
        for first in (0, HALF):
            span = slice(first, first + HALF)
            gap = run_t[:, span] - run_col[head, span, :]
            levels = level_of[...]
            chosen = jnp.zeros((HALF, HALF), f32)
            for rank in range(SPAN_BITS):
                chosen = jnp.where(levels == rank, mixes[rank][:, span], chosen)
            weights.append(chosen * jnp.exp(jnp.minimum(gap, 0.0)) * scores[span, span])
        gap = run_t[:, HALF:] - run_col[head, :HALF, :]
        cross = mixes[SPAN_BITS][:, HALF:] * jnp.exp(jnp.minimum(gap, 0.0))
        cross = (cross * scores[:HALF, HALF:]).astype(bf16)
        rows = rows_of(head, head_dim)
        mixed[rows, :HALF] = jnp.dot(
            values[:, :HALF], weights[0].astype(bf16), preferred_element_type=f32
        )
        mixed[rows, HALF:] = jnp.dot(
            values, jnp.concatenate([cross, weights[1].astype(bf16)]), preferred_element_type=f32
        )
        return 0

    def locals_of(quarter):
        lax.fori_loop(quarter * heads // 4, (quarter + 1) * heads // 4, local, 0)

    prefix = jnp.zeros((heads, 128), f32)

    def scale_level(bit, prefix):
        upper = (seq // 2**bit % 2).astype(f32)
        growth = jnp.exp(run_row[...] + jnp.concatenate([prefix] * 2, axis=1))
        level_scale[bit] = upper * mix[SPAN_BITS + 1 + bit] * growth

    def merge(bit, total, prefix):
        for copy in rounds[bit]:
            copy.wait_recv()
        other = decay_in[bit]
        upper = (seq // 2**bit % 2).astype(f32)
        scale_level(bit, prefix)
        tail[:, :128] = jnp.exp((1.0 - upper) * other)
        tail[:, 128:] = jnp.exp(upper * total)

        def add(head, _):
            rows = rows_of(head, head_dim)
            factors = tail[pl.ds(head, 1), :]
            mine = factors[:, :128] * state[rows, :]
            both = mine + factors[:, 128:] * state_in[bit, rows, :].astype(f32)
            state[rows, :] = both
            state_out[bit + 1, rows, :] = both.astype(bf16)
            return 0

        lax.fori_loop(0, heads, add, 0)
        total = total + other
        if bit == 0:
            decay_out[1] = total
        rounds.append(exchange(bit + 1))
        for copy in rounds[bit + 1]:
            copy.start()
        return total, prefix + upper * other

    def distant(bit):
        def add(index, _):
            rows = rows_of(index, GROUP * head_dim)
            product = lax.dot_general(
                state_in[bit, rows, :], queries[...], NT, preferred_element_type=f32
            )
            for place in range(GROUP):
                head = index * GROUP + place
                part = product[place * head_dim : (place + 1) * head_dim]
                mixed[rows_of(head, head_dim), :] += level_scale[bit, pl.ds(head, 1), :] * part
            return 0

        lax.fori_loop(0, heads // GROUP, add, 0)

    locals_of(0)
    gather.line(2, 0)
    total, prefix = merge(0, total, prefix)
    gather.across(1, 0)
    locals_of(1)
    gather.line(2, 1)
    gather.across(1, 1)
    locals_of(2)
    gather.line(3, 0)
    gather.corner(0)
    total, prefix = merge(1, total, prefix)
    scale_level(2, prefix)
    gather.line(3, 1)
    gather.across(2, 0)
    locals_of(3)
    gather.corner(1)
    gather.across(2, 1)
    distant(0)
    distant(1)

    def turn_gate(index, _):
        lanes = rows_of(index, 128)
        gate_cols[lanes, :] = gate_in[:, lanes].astype(f32).T.astype(bf16)
        return 0

    lax.fori_loop(0, gate_cols.shape[0] // 128, turn_gate, 0)
    gather.across(3, 0)
    gather.across(3, 1)
    rounds[2][0].wait_recv()
    distant(2)

    def gated(index, squares):
        rows = rows_of(index, head_dim)
        gate = gate_cols[rows, :].astype(f32)
        value = mixed[rows, :] * (gate / (1.0 + jnp.exp(-gate)))
        mixed[rows, :] = value
        return squares + jnp.sum(value * value, axis=0, keepdims=True)

    squares = lax.fori_loop(0, heads, gated, jnp.zeros((1, SPAN), f32))
    scale = lax.rsqrt(squares / mixed.shape[0] + EPS)

    def norm(index, _):
        rows = rows_of(index, head_dim)
        normed[rows, :] = (mixed[rows, :] * scale * gain[rows, :]).astype(bf16)
        return 0

    lax.fori_loop(0, heads, norm, 0)

    def project(chip):
        gate = jnp.dot(held[0, chip], normed[...], preferred_element_type=f32)
        up = jnp.dot(held[1, chip], normed[...], preferred_element_type=f32)
        hidden[chip] = (gate / (1.0 + jnp.exp(-gate)) * up).astype(bf16)

    gather.own.wait()
    for step in range(LINE - 1):
        for kind in range(4):
            if (step, kind) != (2, 3):
                project(gather.ready(step, kind))
    gather.corner(2)
    for kind in range(3):
        project(gather.ready(3, kind))
    project(gather.ready(2, 3))
    gather.corner(3)
    project(gather.ready(3, 3))
    gather.finish()
    for copies in rounds:
        for copy in copies:
            copy.wait_send()


def chip_rows(w_gate, w_up):
    first = lax.axis_index("dp") % 2 == 0
    gate, up = w_gate.T, w_up.T
    pairs = [(source, source ^ 1) for source in range(DP_COUNT)]
    other = lax.ppermute(jnp.where(first, up, gate), "dp", pairs)
    return jnp.where(first, jnp.concatenate([gate, other]), jnp.concatenate([other, up]))


def streamed_layer(x, gate, keys, queries, decay, mix, norm_gain, w_gate, w_up):
    piece = chip_rows(w_gate, w_up)
    rows, depth = piece.shape
    tokens = x.shape[0]
    heads = decay.shape[0]
    states = keys.shape[1]
    sems = pltpu.SemaphoreType.DMA
    f32, bf16 = jnp.float32, jnp.bfloat16
    hidden = pl.pallas_call(
        layer_kernel,
        out_shape=jax.ShapeDtypeStruct((CHIPS, rows, tokens), bf16),
        in_specs=[pl.BlockSpec(memory_space=pltpu.VMEM)] * 8,
        out_specs=pl.BlockSpec(memory_space=pltpu.VMEM),
        scratch_shapes=[
            pltpu.VMEM((2, CHIPS, rows, depth), bf16),
            pltpu.VMEM((depth, tokens), bf16),
            pltpu.VMEM((depth, tokens), bf16),
            pltpu.VMEM((depth, tokens), bf16),
            pltpu.VMEM((depth, tokens), f32),
            pltpu.VMEM((heads, tokens, 128), f32),
            pltpu.VMEM((heads, tokens), f32),
            pltpu.VMEM((heads, tokens), f32),
            pltpu.VMEM((3, heads, tokens), f32),
            pltpu.VMEM((HALF, HALF), jnp.int32),
            pltpu.VMEM((SPAN, SPAN), f32),
            pltpu.VMEM((depth, states), f32),
            pltpu.VMEM((3, depth, states), bf16),
            pltpu.VMEM((3, depth, states), bf16),
            pltpu.VMEM((2, heads, 128), f32),
            pltpu.VMEM((2, heads, 128), f32),
            sems((2, 6)),
            sems((2, 12)),
            sems((2, 12)),
            sems((2, 2 * CHIPS)),
            sems,
            sems((2, 3)),
            sems((2, 2)),
        ],
        compiler_params=pltpu.CompilerParams(
            collective_id=0, has_side_effects=True, vmem_limit_bytes=56 * 2**20
        ),
        cost_estimate=pl.CostEstimate(
            flops=4 * tokens * CHIPS * rows * depth,
            bytes_accessed=2 * CHIPS * rows * depth * 2,
            transcendentals=tokens * CHIPS * rows,
        ),
    )(x, gate, keys, queries, decay, mix, norm_gain[:, None], piece)
    return hidden.reshape(CHIPS * rows, tokens).T


def per_device(x_in, gate_in, keys_b, queries_c, decay_log, level_mix, norm_gain, w_gate, w_up):
    mesh_sizes = (lax.axis_size("seq"), lax.axis_size("dp"))
    if mesh_sizes == (SEQ_COUNT, DP_COUNT) and x_in.shape[1] == SPAN:
        local = (x_in, gate_in, keys_b, queries_c, decay_log, level_mix)
        layer = streamed_layer(*(array[0] for array in local), norm_gain, w_gate, w_up)
        return layer[None]
    tok_dev = x_in.shape[1]
    embedding_width = x_in.shape[2]
    head_count = decay_log.shape[1]
    head_dim = embedding_width // head_count
    blocks = tok_dev // SPAN
    inner_count = SPAN_BITS + 1
    seq_bits = lax.axis_size("seq").bit_length() - 1
    x_blocks = x_in[0].reshape(blocks, SPAN, head_count, head_dim)
    b_blocks = keys_b[0].reshape(blocks, SPAN, -1)
    c_blocks = queries_c[0].reshape(blocks, SPAN, -1)
    a_blocks = decay_log[0].reshape(head_count, blocks, SPAN)
    mix_all = level_mix[0].reshape(level_mix.shape[1], head_count, blocks, SPAN)
    local_parts, block_states, block_decays, runnings = ([], [], [], [])
    block_index = 0
    local_part, block_state, running = block_inner(
        x_blocks[block_index],
        b_blocks[block_index],
        c_blocks[block_index],
        a_blocks[:, block_index],
        mix_all[:inner_count, :, block_index],
    )
    local_parts.append(local_part)
    block_states.append(block_state)
    block_decays.append(running[:, -1])
    runnings.append(running)
    summary = jnp.zeros_like(block_states[0])
    block_index = 0
    summary = (
        jnp.exp(block_decays[block_index])[:, None, None] * summary + block_states[block_index]
    )
    summary_decay = block_decays[block_index]
    rank_here = lax.axis_index("seq")
    own_prefix = jnp.zeros((head_count,), jnp.float32)
    device_levels = []
    for bit_index in range(seq_bits):
        other_state, other_decay = swapped((summary.astype(jnp.bfloat16), summary_decay), "seq", bit_index)
        other_state = other_state.astype(jnp.float32)
        is_upper = rank_here >> bit_index & 1 == 1
        device_levels.append(
            jnp.where(is_upper, jnp.exp(own_prefix)[:, None, None] * other_state, 0.0)
        )
        lower_state = jnp.where(is_upper, other_state, summary)
        lower_decay = jnp.where(is_upper, other_decay, summary_decay)
        upper_state = jnp.where(is_upper, summary, other_state)
        upper_decay = jnp.where(is_upper, summary_decay, other_decay)
        summary = jnp.exp(upper_decay)[:, None, None] * lower_state + upper_state
        summary_decay = lower_decay + upper_decay
        own_prefix = jnp.where(is_upper, own_prefix + other_decay, own_prefix)
    zero_decay = jnp.zeros((head_count,), jnp.float32)
    block_index = 0
    levels = []
    lead_decay = sum(block_decays[:block_index], zero_decay)
    for device_level in device_levels:
        levels.append(jnp.exp(lead_decay)[:, None, None] * device_level)
    distant = block_distant(
        c_blocks[block_index], runnings[block_index], mix_all[inner_count:, :, block_index], levels
    )
    outputs = local_parts[block_index] + distant
    mixed = outputs.reshape(tok_dev, embedding_width)
    gated = mixed * jax.nn.silu(gate_in[0].astype(jnp.float32))
    normed = (
        gated * lax.rsqrt(jnp.mean(gated * gated, axis=-1, keepdims=True) + EPS) * norm_gain
    ).astype(jnp.bfloat16)
    return gathered_projection(normed, w_gate, w_up)[None]


def solution(mesh):
    in_specs = (
        P("dp", "seq", None),
        P("dp", "seq", None),
        P("dp", "seq", None),
        P("dp", "seq", None),
        P("dp", None, "seq"),
        P("dp", None, None, "seq"),
        P(),
        P(None, ("seq", "dp")),
        P(None, ("seq", "dp")),
    )
    out_specs = P("dp", "seq", None)
    return jax.shard_map(
        per_device, mesh=mesh, in_specs=in_specs, out_specs=out_specs, check_vma=False
    )
```

```python
import jax
import jax.numpy as jnp
from jax import lax
from jax.experimental import pallas as pl
from jax.experimental.pallas import tpu as pltpu
from jax.sharding import PartitionSpec as P

SPAN = 256
SPAN_BITS = 8


EPS = 1e-05
HIGH = lax.Precision.HIGHEST


def swapped(value, axis, distance):
    mask = 2**distance
    pairs = [(source, source ^ mask) for source in range(lax.axis_size(axis))]
    return lax.ppermute(value, axis, pairs)


def top_bit(values):
    powers = jnp.arange(1, 31, dtype=jnp.int32)
    return jnp.sum(values[..., None] >> powers > 0, axis=-1)


def block_inner(x_blk, b_blk, c_blk, a_blk, mix_low):
    length = a_blk.shape[1]
    inner_count = mix_low.shape[0]
    running = jnp.cumsum(a_blk, axis=1)
    position = jnp.arange(length, dtype=jnp.int32)
    differ = position[:, None] ^ position[None, :]
    level_table = jnp.where(differ > 0, top_bit(differ) + 1, 0)
    level_picks = (
        level_table[None] == jnp.arange(inner_count, dtype=jnp.int32)[:, None, None]
    ).astype(jnp.float32)
    chosen = jnp.einsum("lht,lts->hts", mix_low, level_picks, precision=HIGH)
    causal_mask = position[:, None] >= position[None, :]
    log_gap = jnp.where(causal_mask[None], running[:, :, None] - running[:, None, :], -jnp.inf)
    scores = jnp.dot(c_blk, b_blk.T, preferred_element_type=jnp.float32)
    weights = (chosen * jnp.exp(log_gap) * scores[None]).astype(jnp.bfloat16)
    local_part = jnp.einsum("hts,shp->thp", weights, x_blk, preferred_element_type=jnp.float32)
    tail_decay = jnp.exp(running[:, -1:] - running)
    scaled_keys = (tail_decay.T[:, :, None] * b_blk[:, None, :]).astype(jnp.bfloat16)
    block_state = jnp.einsum("shn,shp->hnp", scaled_keys, x_blk, preferred_element_type=jnp.float32)
    return (local_part, block_state, running)


def block_distant(c_blk, running, mix_high, levels):
    growth = jnp.exp(running)
    distant_sum = jnp.zeros((c_blk.shape[0], running.shape[0], levels[0].shape[2]), jnp.float32)
    for level_rank in range(len(levels)):
        level_scale = (mix_high[level_rank] * growth).T
        product = jnp.einsum(
            "tn,hnp->thp",
            c_blk,
            levels[level_rank].astype(jnp.bfloat16),
            preferred_element_type=jnp.float32,
        )
        distant_sum = distant_sum + level_scale[:, :, None] * product
    return distant_sum


def gathered_projection(normed, w_gate, w_up):
    tok_dev = normed.shape[0]
    paired = jnp.stack([w_gate, w_up])
    dp_count = lax.axis_size("dp")
    seq_count = lax.axis_size("seq")
    seq_weights = lax.all_gather(paired, "seq", axis=2, tiled=True)
    projected = jnp.einsum(
        "td,gdk->gtk",
        normed,
        lax.all_gather(seq_weights, "dp", axis=2, tiled=True),
        preferred_element_type=jnp.float32,
    )
    returned = (jax.nn.silu(projected[0]) * projected[1]).astype(jnp.bfloat16)
    hidden = (
        returned.reshape(tok_dev, dp_count, seq_count, -1)
        .transpose(0, 2, 1, 3)
        .reshape(tok_dev, -1)
    )
    return hidden


MESH = pl.DeviceIdType.MESH
SEQ_COUNT = 8
DP_COUNT = 4
LINE = 4
CHIPS = 16
PARTS = 3


def line_member(z, steps):
    place = z + (z >= 2) * (5 - 2 * z)
    back = lax.rem(place - steps + 2 * LINE, LINE)
    return back + (back >= 2) * (5 - 2 * back)


class Gather:
    def __init__(self, piece, held, z_sems, x_sems, y_sems, core_sems, own_sem):
        self.piece, self.held, self.own_sem = piece, held, own_sem
        self.sems = {"z": z_sems, "x": x_sems, "y": y_sems, "core": core_sems}
        seq, dp = lax.axis_index("seq"), lax.axis_index("dp")
        self.seq, self.dp = seq, dp
        self.z, self.x, self.y, self.core = seq // 2, lax.rem(seq, 2), dp // 2, lax.rem(dp, 2)
        self.targets = {
            "z": (line_member(self.z, -1) * 2 + self.x, dp),
            "x": (self.z * 2 + 1 - self.x, dp),
            "y": (seq, (1 - self.y) * 2 + self.core),
            "core": (seq, self.y * 2 + 1 - self.core),
        }
        self.before = (line_member(self.z, 1) * 2 + self.x, dp)
        rows = piece.shape[0]
        side = (rows // 3 + 15) // 16 * 16
        self.cuts = ((0, side), (side, rows - 2 * side), (rows - side, side))
        self.sent = []

    def greet(self):
        barrier = pltpu.get_barrier_semaphore()
        others = list(self.targets.values()) + [self.before]
        for other in others:
            pl.semaphore_signal(barrier, inc=1, device_id=other, device_id_type=MESH)
        pl.semaphore_wait(barrier, len(others))

    def chip(self, step, flip_x, flip_y):
        x = 1 - self.x if flip_x else self.x
        y = 1 - self.y if flip_y else self.y
        return line_member(self.z, step) * 4 + x * 2 + y

    def copy(self, way, slot, chip, part, own=False):
        first, count = self.cuts[part]
        place = self.held.at[chip, self.core, pl.ds(first, count)]
        return pltpu.make_async_remote_copy(
            src_ref=self.piece.at[pl.ds(first, count)] if own else place,
            dst_ref=place,
            send_sem=self.sems[way].at[0, slot],
            recv_sem=self.sems[way].at[1, slot],
            device_id=self.targets[way],
            device_id_type=MESH,
        )

    def send(self, way, slot, chip, part, own=False):
        copy = self.copy(way, slot, chip, part, own)
        copy.start()
        self.sent.append(copy)

    def start(self):
        chip = self.chip(0, 0, 0)
        self.own = pltpu.make_async_copy(self.piece, self.held.at[chip, self.core], self.own_sem)
        self.own.start()
        for part in range(PARTS):
            for way in ("z", "y"):
                self.send(way, part, chip, part, own=True)
        self.send("x", 0, chip, 0, own=True)

    def start_rest(self):
        chip = self.chip(0, 0, 0)
        for part in range(1, PARTS):
            self.send("x", part, chip, part, own=True)
        for part in range(PARTS):
            self.send("core", part, chip, part, own=True)

    def line(self, step, part):
        chip = self.chip(step, 0, 0)
        self.copy("z", (step - 1) * PARTS + part, chip, part).wait_recv()
        if step < LINE - 1:
            self.send("z", step * PARTS + part, chip, part)
        for way in ("x", "y"):
            self.send(way, step * PARTS + part, chip, part)
        self.send("core", step * 4 * PARTS + part, chip, part)

    def across_x(self, step, part):
        chip = self.chip(step, 1, 0)
        self.copy("x", step * PARTS + part, chip, part).wait_recv()
        if part == 0:
            self.send("y", PARTS * LINE + step, chip, part)
        if part == 2 and step == 0:
            self.send("y", (PARTS + 1) * LINE, chip, part)
        self.send("core", (step * 4 + 1) * PARTS + part, chip, part)

    def across_y(self, step, part):
        chip = self.chip(step, 0, 1)
        self.copy("y", step * PARTS + part, chip, part).wait_recv()
        if part == 1:
            self.send("x", PARTS * LINE + step, chip, part)
        self.send("core", (step * 4 + 2) * PARTS + part, chip, part)

    def across(self, step, part):
        self.across_x(step, part)
        self.across_y(step, part)

    def corner(self, step):
        chip = self.chip(step, 1, 1)
        ways = (
            ("y", PARTS * LINE + step),
            ("x", PARTS * LINE + step),
            ("z", PARTS * (LINE - 1) + step - 1) if step else ("y", (PARTS + 1) * LINE),
        )
        for part in (2, 0, 1):
            way, slot = ways[part]
            self.copy(way, slot, chip, part).wait_recv()
            if part == 2 and step < LINE - 1:
                self.send("z", PARTS * (LINE - 1) + step, chip, part)
            self.send("core", (step * 4 + 3) * PARTS + part, chip, part)

    def ready(self, step, kind):
        chip = self.chip(step, kind % 2, kind // 2)
        for part in range(PARTS):
            first, count = self.cuts[part]
            place = self.held.at[chip, 1 - self.core, pl.ds(first, count)]
            slot = (step * 4 + kind) * PARTS + part
            pltpu.make_async_remote_copy(
                src_ref=place,
                dst_ref=place,
                send_sem=self.sems["core"].at[0, slot],
                recv_sem=self.sems["core"].at[1, slot],
                device_id=self.targets["core"],
                device_id_type=MESH,
            ).wait_recv()
        return chip

    def finish(self):
        for copy in self.sent:
            copy.wait_send()


NT = (((1,), (1,)), ((), ()))
HALF = SPAN // 2
GROUP = 4


def rows_of(index, count):
    return pl.ds(pl.multiple_of(index * count, count), count)


def layer_kernel(
    x_in, gate_in, keys, queries, decay, mix, gain, piece, hidden,
    held, x_cols, gate_cols, gain_cols, normed, mixed, run_col, run_row, tail, level_scale,
    level_of, scores, state, state_out, state_in, decay_out, decay_in,
    z_sems, x_sems, y_sems, core_sems, own_sem, state_sems, decay_sems,
):
    gather = Gather(piece, held, z_sems, x_sems, y_sems, core_sems, own_sem)
    gather.greet()
    gather.start()
    heads = decay.shape[0]
    head_dim = x_cols.shape[0] // heads
    seq, dp = gather.seq, gather.dp
    f32, bf16 = jnp.float32, jnp.bfloat16

    def exchange(bit):
        target = (seq + (1 - 2 * (seq // 2**bit % 2)) * 2**bit, dp)
        pairs = [(state_out, state_in, state_sems), (decay_out, decay_in, decay_sems)]
        return [
            pltpu.make_async_remote_copy(
                src_ref=source.at[bit],
                dst_ref=place.at[bit],
                send_sem=sems.at[0, bit],
                recv_sem=sems.at[1, bit],
                device_id=target,
                device_id_type=MESH,
            )
            for source, place, sems in pairs[: 1 if bit == 2 else 2]
        ]

    before = lax.broadcasted_iota(jnp.int32, (SPAN, SPAN), 0)
    after = lax.broadcasted_iota(jnp.int32, (SPAN, SPAN), 1)
    up_to = (before <= after).astype(f32)
    run = jnp.dot(decay[...], up_to, precision=HIGH, preferred_element_type=f32)
    run_row[...] = run
    tail[...] = jnp.exp(jnp.minimum(run[:, SPAN - 1 :] - run, 0.0))
    total = jnp.broadcast_to(run[:, SPAN - 1 :], (heads, 128))
    decay_out[0] = total

    def turn(index, _):
        lanes = rows_of(index, 128)
        x_cols[lanes, :] = x_in[:, lanes].astype(f32).T.astype(bf16)
        return 0

    lax.fori_loop(0, x_cols.shape[0] // 128, turn, 0)

    def block_states(index, _):
        parts = []
        for place in range(GROUP):
            head = index * GROUP + place
            values = x_cols[rows_of(head, head_dim), :].astype(f32) * tail[pl.ds(head, 1), :]
            parts.append(values.astype(bf16))
        rows = rows_of(index, GROUP * head_dim)
        result = jnp.dot(jnp.concatenate(parts), keys[...], preferred_element_type=f32)
        state[rows, :] = result
        state_out[0, rows, :] = result.astype(bf16)
        return 0

    lax.fori_loop(0, heads // GROUP, block_states, 0)
    rounds = [exchange(0)]
    for copy in rounds[0]:
        copy.start()
    gather.start_rest()

    gather.line(1, 0)
    gather.across(0, 0)

    columns = lax.dot_general(
        (before >= after).astype(f32), decay[...], NT, precision=HIGH, preferred_element_type=f32
    )
    for head in range(heads):
        run_col[head] = jnp.broadcast_to(columns[:, head : head + 1], (SPAN, 128))
    scores[...] = lax.dot_general(keys[...], queries[...], NT, preferred_element_type=f32)
    source = lax.broadcasted_iota(jnp.int32, (HALF, HALF), 0)
    target = lax.broadcasted_iota(jnp.int32, (HALF, HALF), 1)
    differ = source ^ target
    level = jnp.zeros((HALF, HALF), jnp.int32)
    for bit in range(SPAN_BITS - 1):
        level = level + (differ >= 2**bit).astype(jnp.int32)
    level_of[...] = jnp.where(source <= target, level, -1)

    gather.line(1, 1)
    gather.across(0, 1)
    gather.line(1, 2)
    gather.across(0, 2)

    def local(head, _):
        run_t = run_row[pl.ds(head, 1), :]
        mixes = [mix[rank, pl.ds(head, 1), :] for rank in range(SPAN_BITS + 1)]
        values = x_cols[rows_of(head, head_dim), :]
        weights = []
        for first in (0, HALF):
            span = slice(first, first + HALF)
            gap = run_t[:, span] - run_col[head, span, :]
            levels = level_of[...]
            chosen = jnp.zeros((HALF, HALF), f32)
            for rank in range(SPAN_BITS):
                chosen = jnp.where(levels == rank, mixes[rank][:, span], chosen)
            weights.append(chosen * jnp.exp(jnp.minimum(gap, 0.0)) * scores[span, span])
        gap = run_t[:, HALF:] - run_col[head, :HALF, :]
        cross = mixes[SPAN_BITS][:, HALF:] * jnp.exp(jnp.minimum(gap, 0.0))
        cross = (cross * scores[:HALF, HALF:]).astype(bf16)
        rows = rows_of(head, head_dim)
        mixed[rows, :HALF] = jnp.dot(
            values[:, :HALF], weights[0].astype(bf16), preferred_element_type=f32
        )
        mixed[rows, HALF:] = jnp.dot(
            values, jnp.concatenate([cross, weights[1].astype(bf16)]), preferred_element_type=f32
        )
        return 0

    def locals_of(quarter):
        lax.fori_loop(quarter * heads // 4, (quarter + 1) * heads // 4, local, 0)

    prefix = jnp.zeros((heads, 128), f32)

    def scale_level(bit, prefix):
        upper = (seq // 2**bit % 2).astype(f32)
        growth = jnp.exp(run_row[...] + jnp.concatenate([prefix] * 2, axis=1))
        level_scale[bit] = upper * mix[SPAN_BITS + 1 + bit] * growth

    def merge(bit, total, prefix):
        for copy in rounds[bit]:
            copy.wait_recv()
        other = decay_in[bit]
        upper = (seq // 2**bit % 2).astype(f32)
        scale_level(bit, prefix)
        tail[:, :128] = jnp.exp((1.0 - upper) * other)
        tail[:, 128:] = jnp.exp(upper * total)

        def add(head, _):
            rows = rows_of(head, head_dim)
            factors = tail[pl.ds(head, 1), :]
            mine = factors[:, :128] * state[rows, :]
            both = mine + factors[:, 128:] * state_in[bit, rows, :].astype(f32)
            state[rows, :] = both
            state_out[bit + 1, rows, :] = both.astype(bf16)
            return 0

        lax.fori_loop(0, heads, add, 0)
        total = total + other
        if bit == 0:
            decay_out[1] = total
        rounds.append(exchange(bit + 1))
        for copy in rounds[bit + 1]:
            copy.start()
        return total, prefix + upper * other

    def distant(bit):
        def add(index, _):
            rows = rows_of(index, GROUP * head_dim)
            product = lax.dot_general(
                state_in[bit, rows, :], queries[...], NT, preferred_element_type=f32
            )
            for place in range(GROUP):
                head = index * GROUP + place
                part = product[place * head_dim : (place + 1) * head_dim]
                mixed[rows_of(head, head_dim), :] += level_scale[bit, pl.ds(head, 1), :] * part
            return 0

        lax.fori_loop(0, heads // GROUP, add, 0)

    locals_of(0)
    total, prefix = merge(0, total, prefix)
    gather.line(2, 0)
    gather.across(1, 0)
    locals_of(1)
    gather.line(2, 1)
    gather.line(2, 2)
    gather.corner(0)
    locals_of(2)
    gather.across(1, 1)
    gather.across(1, 2)
    gather.line(3, 0)
    total, prefix = merge(1, total, prefix)
    scale_level(2, prefix)
    gather.line(3, 1)
    gather.line(3, 2)
    gather.corner(1)
    locals_of(3)
    gather.across(2, 0)
    distant(0)
    gather.across(2, 1)
    distant(1)
    gather.across(2, 2)

    def turn_gate(index, _):
        lanes = rows_of(index, 128)
        gate_cols[lanes, :] = gate_in[:, lanes].astype(f32).T.astype(bf16)
        gain_cols[lanes, :] = jnp.broadcast_to(gain[:, lanes], (128, 128)).T
        return 0

    lax.fori_loop(0, gate_cols.shape[0] // 128, turn_gate, 0)
    gather.corner(2)
    rounds[2][0].wait_recv()
    distant(2)

    def gated(index, squares):
        rows = rows_of(index, head_dim)
        gate = gate_cols[rows, :].astype(f32)
        value = mixed[rows, :] * (gate / (1.0 + jnp.exp(-gate)))
        mixed[rows, :] = value
        return squares + jnp.sum(value * value, axis=0, keepdims=True)

    squares = lax.fori_loop(0, heads, gated, jnp.zeros((1, SPAN), f32))
    scale = lax.rsqrt(squares / mixed.shape[0] + EPS)

    def norm(index, _):
        rows = rows_of(index, head_dim)
        gains = gain_cols[rows, :]
        value = mixed[rows, :] * scale * jnp.concatenate([gains, gains], axis=1)
        normed[rows, :] = value.astype(bf16)
        return 0

    lax.fori_loop(0, heads, norm, 0)

    rows = piece.shape[0]

    def project(chip, count):
        weights = held[pl.ds(chip, count)].reshape(count * 2 * rows, held.shape[3])
        both = jnp.dot(weights, normed[...], preferred_element_type=f32)
        both = both.reshape(count, 2, rows, SPAN)
        gate, up = both[:, 0], both[:, 1]
        hidden[pl.ds(chip, count)] = (gate / (1.0 + jnp.exp(-gate)) * up).astype(bf16)

    def project_pair(step, kind):
        chip = gather.ready(step, kind)
        gather.ready(step, kind + 2)
        project(chip // 2 * 2, 2)

    gather.own.wait()
    project_pair(0, 0)
    project_pair(0, 1)
    gather.across(3, 0)
    gather.across(3, 1)
    project_pair(1, 0)
    gather.across(3, 2)
    project_pair(1, 1)
    project_pair(2, 0)
    project_pair(2, 1)
    project_pair(3, 0)
    project(gather.ready(3, 1), 1)
    gather.corner(3)
    project(gather.ready(3, 3), 1)
    gather.finish()
    for copies in rounds:
        for copy in copies:
            copy.wait_send()


def chip_rows(w_gate, w_up):
    first = lax.axis_index("dp") % 2 == 0
    gate, up = w_gate.T, w_up.T
    pairs = [(source, source ^ 1) for source in range(DP_COUNT)]
    other = lax.ppermute(jnp.where(first, up, gate), "dp", pairs)
    return jnp.where(first, jnp.concatenate([gate, other]), jnp.concatenate([other, up]))


def streamed_layer(x, gate, keys, queries, decay, mix, norm_gain, w_gate, w_up):
    piece = chip_rows(w_gate, w_up)
    rows, depth = piece.shape
    tokens = x.shape[0]
    heads = decay.shape[0]
    states = keys.shape[1]
    sems = pltpu.SemaphoreType.DMA
    f32, bf16 = jnp.float32, jnp.bfloat16
    hidden = pl.pallas_call(
        layer_kernel,
        out_shape=jax.ShapeDtypeStruct((CHIPS, rows, tokens), bf16),
        in_specs=[pl.BlockSpec(memory_space=pltpu.VMEM)] * 8,
        out_specs=pl.BlockSpec(memory_space=pltpu.VMEM),
        scratch_shapes=[
            pltpu.VMEM((CHIPS, 2, rows, depth), bf16),
            pltpu.VMEM((depth, tokens), bf16),
            pltpu.VMEM((depth, tokens), bf16),
            pltpu.VMEM((depth, 128), f32),
            pltpu.VMEM((depth, tokens), bf16),
            pltpu.VMEM((depth, tokens), f32),
            pltpu.VMEM((heads, tokens, 128), f32),
            pltpu.VMEM((heads, tokens), f32),
            pltpu.VMEM((heads, tokens), f32),
            pltpu.VMEM((3, heads, tokens), f32),
            pltpu.VMEM((HALF, HALF), jnp.int32),
            pltpu.VMEM((SPAN, SPAN), f32),
            pltpu.VMEM((depth, states), f32),
            pltpu.VMEM((3, depth, states), bf16),
            pltpu.VMEM((3, depth, states), bf16),
            pltpu.VMEM((2, heads, 128), f32),
            pltpu.VMEM((2, heads, 128), f32),
            sems((2, (PARTS + 1) * (LINE - 1))),
            sems((2, (PARTS + 1) * LINE)),
            sems((2, (PARTS + 1) * LINE + 1)),
            sems((2, PARTS * CHIPS)),
            sems,
            sems((2, 3)),
            sems((2, 2)),
        ],
        compiler_params=pltpu.CompilerParams(
            collective_id=0, has_side_effects=True, vmem_limit_bytes=56 * 2**20
        ),
        cost_estimate=pl.CostEstimate(
            flops=4 * tokens * CHIPS * rows * depth,
            bytes_accessed=2 * CHIPS * rows * depth * 2,
            transcendentals=tokens * CHIPS * rows,
        ),
    )(x, gate, keys, queries, decay, mix, norm_gain[None, :], piece)
    return hidden.reshape(CHIPS * rows, tokens).T


def per_device(x_in, gate_in, keys_b, queries_c, decay_log, level_mix, norm_gain, w_gate, w_up):
    mesh_sizes = (lax.axis_size("seq"), lax.axis_size("dp"))
    if mesh_sizes == (SEQ_COUNT, DP_COUNT) and x_in.shape[1] == SPAN:
        local = (x_in, gate_in, keys_b, queries_c, decay_log, level_mix)
        layer = streamed_layer(*(array[0] for array in local), norm_gain, w_gate, w_up)
        return layer[None]
    tok_dev = x_in.shape[1]
    embedding_width = x_in.shape[2]
    head_count = decay_log.shape[1]
    head_dim = embedding_width // head_count
    blocks = tok_dev // SPAN
    inner_count = SPAN_BITS + 1
    seq_bits = lax.axis_size("seq").bit_length() - 1
    x_blocks = x_in[0].reshape(blocks, SPAN, head_count, head_dim)
    b_blocks = keys_b[0].reshape(blocks, SPAN, -1)
    c_blocks = queries_c[0].reshape(blocks, SPAN, -1)
    a_blocks = decay_log[0].reshape(head_count, blocks, SPAN)
    mix_all = level_mix[0].reshape(level_mix.shape[1], head_count, blocks, SPAN)
    local_parts, block_states, block_decays, runnings = ([], [], [], [])
    block_index = 0
    local_part, block_state, running = block_inner(
        x_blocks[block_index],
        b_blocks[block_index],
        c_blocks[block_index],
        a_blocks[:, block_index],
        mix_all[:inner_count, :, block_index],
    )
    local_parts.append(local_part)
    block_states.append(block_state)
    block_decays.append(running[:, -1])
    runnings.append(running)
    summary = jnp.zeros_like(block_states[0])
    block_index = 0
    summary = (
        jnp.exp(block_decays[block_index])[:, None, None] * summary + block_states[block_index]
    )
    summary_decay = block_decays[block_index]
    rank_here = lax.axis_index("seq")
    own_prefix = jnp.zeros((head_count,), jnp.float32)
    device_levels = []
    for bit_index in range(seq_bits):
        other_state, other_decay = swapped((summary.astype(jnp.bfloat16), summary_decay), "seq", bit_index)
        other_state = other_state.astype(jnp.float32)
        is_upper = rank_here >> bit_index & 1 == 1
        device_levels.append(
            jnp.where(is_upper, jnp.exp(own_prefix)[:, None, None] * other_state, 0.0)
        )
        lower_state = jnp.where(is_upper, other_state, summary)
        lower_decay = jnp.where(is_upper, other_decay, summary_decay)
        upper_state = jnp.where(is_upper, summary, other_state)
        upper_decay = jnp.where(is_upper, summary_decay, other_decay)
        summary = jnp.exp(upper_decay)[:, None, None] * lower_state + upper_state
        summary_decay = lower_decay + upper_decay
        own_prefix = jnp.where(is_upper, own_prefix + other_decay, own_prefix)
    zero_decay = jnp.zeros((head_count,), jnp.float32)
    block_index = 0
    levels = []
    lead_decay = sum(block_decays[:block_index], zero_decay)
    for device_level in device_levels:
        levels.append(jnp.exp(lead_decay)[:, None, None] * device_level)
    distant = block_distant(
        c_blocks[block_index], runnings[block_index], mix_all[inner_count:, :, block_index], levels
    )
    outputs = local_parts[block_index] + distant
    mixed = outputs.reshape(tok_dev, embedding_width)
    gated = mixed * jax.nn.silu(gate_in[0].astype(jnp.float32))
    normed = (
        gated * lax.rsqrt(jnp.mean(gated * gated, axis=-1, keepdims=True) + EPS) * norm_gain
    ).astype(jnp.bfloat16)
    return gathered_projection(normed, w_gate, w_up)[None]


def solution(mesh):
    in_specs = (
        P("dp", "seq", None),
        P("dp", "seq", None),
        P("dp", "seq", None),
        P("dp", "seq", None),
        P("dp", None, "seq"),
        P("dp", None, None, "seq"),
        P(),
        P(None, ("seq", "dp")),
        P(None, ("seq", "dp")),
    )
    out_specs = P("dp", "seq", None)
    return jax.shard_map(
        per_device, mesh=mesh, in_specs=in_specs, out_specs=out_specs, check_vma=False
    )
```

```python
import jax
import jax.numpy as jnp
from jax import lax
from jax.experimental import pallas as pl
from jax.experimental.pallas import tpu as pltpu
from jax.sharding import PartitionSpec as P

SPAN = 256
SPAN_BITS = 8


EPS = 1e-05
HIGH = lax.Precision.HIGHEST


def swapped(value, axis, distance):
    mask = 2**distance
    pairs = [(source, source ^ mask) for source in range(lax.axis_size(axis))]
    return lax.ppermute(value, axis, pairs)


def top_bit(values):
    powers = jnp.arange(1, 31, dtype=jnp.int32)
    return jnp.sum(values[..., None] >> powers > 0, axis=-1)


def block_inner(x_blk, b_blk, c_blk, a_blk, mix_low):
    length = a_blk.shape[1]
    inner_count = mix_low.shape[0]
    running = jnp.cumsum(a_blk, axis=1)
    position = jnp.arange(length, dtype=jnp.int32)
    differ = position[:, None] ^ position[None, :]
    level_table = jnp.where(differ > 0, top_bit(differ) + 1, 0)
    level_picks = (
        level_table[None] == jnp.arange(inner_count, dtype=jnp.int32)[:, None, None]
    ).astype(jnp.float32)
    chosen = jnp.einsum("lht,lts->hts", mix_low, level_picks, precision=HIGH)
    causal_mask = position[:, None] >= position[None, :]
    log_gap = jnp.where(causal_mask[None], running[:, :, None] - running[:, None, :], -jnp.inf)
    scores = jnp.dot(c_blk, b_blk.T, preferred_element_type=jnp.float32)
    weights = (chosen * jnp.exp(log_gap) * scores[None]).astype(jnp.bfloat16)
    local_part = jnp.einsum("hts,shp->thp", weights, x_blk, preferred_element_type=jnp.float32)
    tail_decay = jnp.exp(running[:, -1:] - running)
    scaled_keys = (tail_decay.T[:, :, None] * b_blk[:, None, :]).astype(jnp.bfloat16)
    block_state = jnp.einsum("shn,shp->hnp", scaled_keys, x_blk, preferred_element_type=jnp.float32)
    return (local_part, block_state, running)


def block_distant(c_blk, running, mix_high, levels):
    growth = jnp.exp(running)
    distant_sum = jnp.zeros((c_blk.shape[0], running.shape[0], levels[0].shape[2]), jnp.float32)
    for level_rank in range(len(levels)):
        level_scale = (mix_high[level_rank] * growth).T
        product = jnp.einsum(
            "tn,hnp->thp",
            c_blk,
            levels[level_rank].astype(jnp.bfloat16),
            preferred_element_type=jnp.float32,
        )
        distant_sum = distant_sum + level_scale[:, :, None] * product
    return distant_sum


def gathered_projection(normed, w_gate, w_up):
    tok_dev = normed.shape[0]
    paired = jnp.stack([w_gate, w_up])
    dp_count = lax.axis_size("dp")
    seq_count = lax.axis_size("seq")
    seq_weights = lax.all_gather(paired, "seq", axis=2, tiled=True)
    projected = jnp.einsum(
        "td,gdk->gtk",
        normed,
        lax.all_gather(seq_weights, "dp", axis=2, tiled=True),
        preferred_element_type=jnp.float32,
    )
    returned = (jax.nn.silu(projected[0]) * projected[1]).astype(jnp.bfloat16)
    hidden = (
        returned.reshape(tok_dev, dp_count, seq_count, -1)
        .transpose(0, 2, 1, 3)
        .reshape(tok_dev, -1)
    )
    return hidden


MESH = pl.DeviceIdType.MESH
SEQ_COUNT = 8
DP_COUNT = 4
LINE = 4
CHIPS = 16


def line_member(z, steps):
    place = z + (z >= 2) * (5 - 2 * z)
    back = lax.rem(place - steps + 2 * LINE, LINE)
    return back + (back >= 2) * (5 - 2 * back)


class Gather:
    def __init__(self, piece, held, z_sems, x_sems, y_sems, core_sems, own_sem):
        self.piece, self.held, self.own_sem = piece, held, own_sem
        self.sems = {"z": z_sems, "x": x_sems, "y": y_sems, "core": core_sems}
        seq, dp = lax.axis_index("seq"), lax.axis_index("dp")
        self.seq, self.dp = seq, dp
        self.z, self.x, self.y, self.core = seq // 2, lax.rem(seq, 2), dp // 2, lax.rem(dp, 2)
        self.targets = {
            "z": (line_member(self.z, -1) * 2 + self.x, dp),
            "x": (self.z * 2 + 1 - self.x, dp),
            "y": (seq, (1 - self.y) * 2 + self.core),
            "core": (seq, self.y * 2 + 1 - self.core),
        }
        self.before = (line_member(self.z, 1) * 2 + self.x, dp)
        rows = piece.shape[0]
        cut = (rows // 2 + 15) // 16 * 16
        self.cuts = ((0, cut), (cut, rows - cut))
        self.sent = []

    def greet(self):
        barrier = pltpu.get_barrier_semaphore()
        others = list(self.targets.values()) + [self.before]
        for other in others:
            pl.semaphore_signal(barrier, inc=1, device_id=other, device_id_type=MESH)
        pl.semaphore_wait(barrier, len(others))

    def chip(self, step, flip_x, flip_y):
        x = 1 - self.x if flip_x else self.x
        y = 1 - self.y if flip_y else self.y
        return line_member(self.z, step) * 4 + x * 2 + y

    def copy(self, way, slot, chip, part, own=False):
        first, count = self.cuts[part]
        place = self.held.at[self.core, chip, pl.ds(first, count)]
        return pltpu.make_async_remote_copy(
            src_ref=self.piece.at[pl.ds(first, count)] if own else place,
            dst_ref=place,
            send_sem=self.sems[way].at[0, slot],
            recv_sem=self.sems[way].at[1, slot],
            device_id=self.targets[way],
            device_id_type=MESH,
        )

    def send(self, way, slot, chip, part, own=False):
        copy = self.copy(way, slot, chip, part, own)
        copy.start()
        self.sent.append(copy)

    def start(self):
        chip = self.chip(0, 0, 0)
        self.own = pltpu.make_async_copy(self.piece, self.held.at[self.core, chip], self.own_sem)
        self.own.start()
        for part in range(2):
            for way in ("z", "y"):
                self.send(way, part, chip, part, own=True)
        self.send("x", 0, chip, 0, own=True)

    def start_rest(self):
        chip = self.chip(0, 0, 0)
        self.send("x", 1, chip, 1, own=True)
        for part in range(2):
            self.send("core", part, chip, part, own=True)

    def line(self, step, part):
        chip = self.chip(step, 0, 0)
        self.copy("z", (step - 1) * 2 + part, chip, part).wait_recv()
        if step < LINE - 1:
            self.send("z", step * 2 + part, chip, part)
        for way in ("x", "y"):
            self.send(way, step * 2 + part, chip, part)
        self.send("core", step * 8 + part, chip, part)

    def across_x(self, step, part):
        chip = self.chip(step, 1, 0)
        self.copy("x", step * 2 + part, chip, part).wait_recv()
        if part == 0:
            self.send("y", 2 * LINE + step, chip, part)
        self.send("core", step * 8 + 2 + part, chip, part)

    def across_y(self, step, part):
        chip = self.chip(step, 0, 1)
        self.copy("y", step * 2 + part, chip, part).wait_recv()
        if part == 1:
            self.send("x", 2 * LINE + step, chip, part)
        self.send("core", step * 8 + 4 + part, chip, part)

    def across(self, step, part):
        self.across_x(step, part)
        self.across_y(step, part)

    def corner(self, step):
        chip = self.chip(step, 1, 1)
        for part, way in enumerate(("y", "x")):
            self.copy(way, 2 * LINE + step, chip, part).wait_recv()
            self.send("core", step * 8 + 6 + part, chip, part)

    def ready(self, step, kind):
        chip = self.chip(step, kind % 2, kind // 2)
        for part in range(2):
            first, count = self.cuts[part]
            place = self.held.at[1 - self.core, chip, pl.ds(first, count)]
            slot = step * 8 + kind * 2 + part
            pltpu.make_async_remote_copy(
                src_ref=place,
                dst_ref=place,
                send_sem=self.sems["core"].at[0, slot],
                recv_sem=self.sems["core"].at[1, slot],
                device_id=self.targets["core"],
                device_id_type=MESH,
            ).wait_recv()
        return chip

    def finish(self):
        for copy in self.sent:
            copy.wait_send()


NT = (((1,), (1,)), ((), ()))
HALF = SPAN // 2
GROUP = 4


def rows_of(index, count):
    return pl.ds(pl.multiple_of(index * count, count), count)


def layer_kernel(
    x_in, gate_in, keys, queries, decay, mix, gain, piece, hidden,
    held, x_cols, gate_cols, gain_cols, normed, mixed, run_col, run_row, tail, level_scale,
    level_of, scores, state, state_out, state_in, decay_out, decay_in,
    z_sems, x_sems, y_sems, core_sems, own_sem, state_sems, decay_sems,
):
    gather = Gather(piece, held, z_sems, x_sems, y_sems, core_sems, own_sem)
    gather.greet()
    gather.start()
    heads = decay.shape[0]
    head_dim = x_cols.shape[0] // heads
    seq, dp = gather.seq, gather.dp
    f32, bf16 = jnp.float32, jnp.bfloat16

    def exchange(bit):
        target = (seq + (1 - 2 * (seq // 2**bit % 2)) * 2**bit, dp)
        pairs = [(state_out, state_in, state_sems), (decay_out, decay_in, decay_sems)]
        return [
            pltpu.make_async_remote_copy(
                src_ref=source.at[bit],
                dst_ref=place.at[bit],
                send_sem=sems.at[0, bit],
                recv_sem=sems.at[1, bit],
                device_id=target,
                device_id_type=MESH,
            )
            for source, place, sems in pairs[: 1 if bit == 2 else 2]
        ]

    before = lax.broadcasted_iota(jnp.int32, (SPAN, SPAN), 0)
    after = lax.broadcasted_iota(jnp.int32, (SPAN, SPAN), 1)
    up_to = (before <= after).astype(f32)
    run = jnp.dot(decay[...], up_to, precision=HIGH, preferred_element_type=f32)
    run_row[...] = run
    tail[...] = jnp.exp(jnp.minimum(run[:, SPAN - 1 :] - run, 0.0))
    total = jnp.broadcast_to(run[:, SPAN - 1 :], (heads, 128))
    decay_out[0] = total

    def turn(index, _):
        lanes = rows_of(index, 128)
        x_cols[lanes, :] = x_in[:, lanes].astype(f32).T.astype(bf16)
        return 0

    lax.fori_loop(0, x_cols.shape[0] // 128, turn, 0)

    def block_states(index, _):
        parts = []
        for place in range(GROUP):
            head = index * GROUP + place
            values = x_cols[rows_of(head, head_dim), :].astype(f32) * tail[pl.ds(head, 1), :]
            parts.append(values.astype(bf16))
        rows = rows_of(index, GROUP * head_dim)
        result = jnp.dot(jnp.concatenate(parts), keys[...], preferred_element_type=f32)
        state[rows, :] = result
        state_out[0, rows, :] = result.astype(bf16)
        return 0

    lax.fori_loop(0, heads // GROUP, block_states, 0)
    rounds = [exchange(0)]
    for copy in rounds[0]:
        copy.start()
    gather.start_rest()

    gather.line(1, 0)
    gather.across(0, 0)

    columns = lax.dot_general(
        (before >= after).astype(f32), decay[...], NT, precision=HIGH, preferred_element_type=f32
    )
    for head in range(heads):
        run_col[head] = jnp.broadcast_to(columns[:, head : head + 1], (SPAN, 128))
    scores[...] = lax.dot_general(keys[...], queries[...], NT, preferred_element_type=f32)
    source = lax.broadcasted_iota(jnp.int32, (HALF, HALF), 0)
    target = lax.broadcasted_iota(jnp.int32, (HALF, HALF), 1)
    differ = source ^ target
    level = jnp.zeros((HALF, HALF), jnp.int32)
    for bit in range(SPAN_BITS - 1):
        level = level + (differ >= 2**bit).astype(jnp.int32)
    level_of[...] = jnp.where(source <= target, level, -1)

    gather.line(1, 1)
    gather.across(0, 1)

    def local(head, _):
        run_t = run_row[pl.ds(head, 1), :]
        mixes = [mix[rank, pl.ds(head, 1), :] for rank in range(SPAN_BITS + 1)]
        values = x_cols[rows_of(head, head_dim), :]
        weights = []
        for first in (0, HALF):
            span = slice(first, first + HALF)
            gap = run_t[:, span] - run_col[head, span, :]
            levels = level_of[...]
            chosen = jnp.zeros((HALF, HALF), f32)
            for rank in range(SPAN_BITS):
                chosen = jnp.where(levels == rank, mixes[rank][:, span], chosen)
            weights.append(chosen * jnp.exp(jnp.minimum(gap, 0.0)) * scores[span, span])
        gap = run_t[:, HALF:] - run_col[head, :HALF, :]
        cross = mixes[SPAN_BITS][:, HALF:] * jnp.exp(jnp.minimum(gap, 0.0))
        cross = (cross * scores[:HALF, HALF:]).astype(bf16)
        rows = rows_of(head, head_dim)
        mixed[rows, :HALF] = jnp.dot(
            values[:, :HALF], weights[0].astype(bf16), preferred_element_type=f32
        )
        mixed[rows, HALF:] = jnp.dot(
            values, jnp.concatenate([cross, weights[1].astype(bf16)]), preferred_element_type=f32
        )
        return 0

    def locals_of(quarter):
        lax.fori_loop(quarter * heads // 4, (quarter + 1) * heads // 4, local, 0)

    prefix = jnp.zeros((heads, 128), f32)

    def scale_level(bit, prefix):
        upper = (seq // 2**bit % 2).astype(f32)
        growth = jnp.exp(run_row[...] + jnp.concatenate([prefix] * 2, axis=1))
        level_scale[bit] = upper * mix[SPAN_BITS + 1 + bit] * growth

    def merge(bit, total, prefix):
        for copy in rounds[bit]:
            copy.wait_recv()
        other = decay_in[bit]
        upper = (seq // 2**bit % 2).astype(f32)
        scale_level(bit, prefix)
        tail[:, :128] = jnp.exp((1.0 - upper) * other)
        tail[:, 128:] = jnp.exp(upper * total)

        def add(head, _):
            rows = rows_of(head, head_dim)
            factors = tail[pl.ds(head, 1), :]
            mine = factors[:, :128] * state[rows, :]
            both = mine + factors[:, 128:] * state_in[bit, rows, :].astype(f32)
            state[rows, :] = both
            state_out[bit + 1, rows, :] = both.astype(bf16)
            return 0

        lax.fori_loop(0, heads, add, 0)
        total = total + other
        if bit == 0:
            decay_out[1] = total
        rounds.append(exchange(bit + 1))
        for copy in rounds[bit + 1]:
            copy.start()
        return total, prefix + upper * other

    def distant(bit):
        def add(index, _):
            rows = rows_of(index, GROUP * head_dim)
            product = lax.dot_general(
                state_in[bit, rows, :], queries[...], NT, preferred_element_type=f32
            )
            for place in range(GROUP):
                head = index * GROUP + place
                part = product[place * head_dim : (place + 1) * head_dim]
                mixed[rows_of(head, head_dim), :] += level_scale[bit, pl.ds(head, 1), :] * part
            return 0

        lax.fori_loop(0, heads // GROUP, add, 0)

    locals_of(0)
    total, prefix = merge(0, total, prefix)
    gather.line(2, 0)
    gather.across(1, 0)
    locals_of(1)
    gather.line(2, 1)
    gather.across(1, 1)
    locals_of(2)
    total, prefix = merge(1, total, prefix)
    scale_level(2, prefix)
    gather.line(3, 0)
    gather.corner(0)
    locals_of(3)
    gather.line(3, 1)
    distant(0)
    gather.across(2, 0)
    distant(1)
    gather.corner(1)

    def turn_gate(index, _):
        lanes = rows_of(index, 128)
        gate_cols[lanes, :] = gate_in[:, lanes].astype(f32).T.astype(bf16)
        gain_cols[lanes, :] = jnp.broadcast_to(gain[:, lanes], (128, 128)).T
        return 0

    lax.fori_loop(0, gate_cols.shape[0] // 128, turn_gate, 0)
    gather.across(2, 1)
    rounds[2][0].wait_recv()
    distant(2)

    def gated(index, squares):
        rows = rows_of(index, head_dim)
        gate = gate_cols[rows, :].astype(f32)
        value = mixed[rows, :] * (gate / (1.0 + jnp.exp(-gate)))
        mixed[rows, :] = value
        return squares + jnp.sum(value * value, axis=0, keepdims=True)

    squares = lax.fori_loop(0, heads, gated, jnp.zeros((1, SPAN), f32))
    scale = lax.rsqrt(squares / mixed.shape[0] + EPS)

    def norm(index, _):
        rows = rows_of(index, head_dim)
        gains = gain_cols[rows, :]
        value = mixed[rows, :] * scale * jnp.concatenate([gains, gains], axis=1)
        normed[rows, :] = value.astype(bf16)
        return 0

    lax.fori_loop(0, heads, norm, 0)

    def project(chip):
        gate = jnp.dot(held[0, chip], normed[...], preferred_element_type=f32)
        up = jnp.dot(held[1, chip], normed[...], preferred_element_type=f32)
        hidden[chip] = (gate / (1.0 + jnp.exp(-gate)) * up).astype(bf16)

    gather.own.wait()
    for kind in range(4):
        project(gather.ready(0, kind))
    gather.across(3, 0)
    for kind in range(4):
        project(gather.ready(1, kind))
    gather.across(3, 1)
    for kind in range(3):
        project(gather.ready(2, kind))
    gather.corner(2)
    project(gather.ready(2, 3))
    for kind in range(3):
        project(gather.ready(3, kind))
    gather.corner(3)
    project(gather.ready(3, 3))
    gather.finish()
    for copies in rounds:
        for copy in copies:
            copy.wait_send()


def chip_rows(w_gate, w_up):
    first = lax.axis_index("dp") % 2 == 0
    gate, up = w_gate.T, w_up.T
    pairs = [(source, source ^ 1) for source in range(DP_COUNT)]
    other = lax.ppermute(jnp.where(first, up, gate), "dp", pairs)
    return jnp.where(first, jnp.concatenate([gate, other]), jnp.concatenate([other, up]))


def streamed_layer(x, gate, keys, queries, decay, mix, norm_gain, w_gate, w_up):
    piece = chip_rows(w_gate, w_up)
    rows, depth = piece.shape
    tokens = x.shape[0]
    heads = decay.shape[0]
    states = keys.shape[1]
    sems = pltpu.SemaphoreType.DMA
    f32, bf16 = jnp.float32, jnp.bfloat16
    hidden = pl.pallas_call(
        layer_kernel,
        out_shape=jax.ShapeDtypeStruct((CHIPS, rows, tokens), bf16),
        in_specs=[pl.BlockSpec(memory_space=pltpu.VMEM)] * 8,
        out_specs=pl.BlockSpec(memory_space=pltpu.VMEM),
        scratch_shapes=[
            pltpu.VMEM((2, CHIPS, rows, depth), bf16),
            pltpu.VMEM((depth, tokens), bf16),
            pltpu.VMEM((depth, tokens), bf16),
            pltpu.VMEM((depth, 128), f32),
            pltpu.VMEM((depth, tokens), bf16),
            pltpu.VMEM((depth, tokens), f32),
            pltpu.VMEM((heads, tokens, 128), f32),
            pltpu.VMEM((heads, tokens), f32),
            pltpu.VMEM((heads, tokens), f32),
            pltpu.VMEM((3, heads, tokens), f32),
            pltpu.VMEM((HALF, HALF), jnp.int32),
            pltpu.VMEM((SPAN, SPAN), f32),
            pltpu.VMEM((depth, states), f32),
            pltpu.VMEM((3, depth, states), bf16),
            pltpu.VMEM((3, depth, states), bf16),
            pltpu.VMEM((2, heads, 128), f32),
            pltpu.VMEM((2, heads, 128), f32),
            sems((2, 6)),
            sems((2, 12)),
            sems((2, 12)),
            sems((2, 2 * CHIPS)),
            sems,
            sems((2, 3)),
            sems((2, 2)),
        ],
        compiler_params=pltpu.CompilerParams(
            collective_id=0, has_side_effects=True, vmem_limit_bytes=56 * 2**20
        ),
        cost_estimate=pl.CostEstimate(
            flops=4 * tokens * CHIPS * rows * depth,
            bytes_accessed=2 * CHIPS * rows * depth * 2,
            transcendentals=tokens * CHIPS * rows,
        ),
    )(x, gate, keys, queries, decay, mix, norm_gain[None, :], piece)
    return hidden.reshape(CHIPS * rows, tokens).T


def per_device(x_in, gate_in, keys_b, queries_c, decay_log, level_mix, norm_gain, w_gate, w_up):
    mesh_sizes = (lax.axis_size("seq"), lax.axis_size("dp"))
    if mesh_sizes == (SEQ_COUNT, DP_COUNT) and x_in.shape[1] == SPAN:
        local = (x_in, gate_in, keys_b, queries_c, decay_log, level_mix)
        layer = streamed_layer(*(array[0] for array in local), norm_gain, w_gate, w_up)
        return layer[None]
    tok_dev = x_in.shape[1]
    embedding_width = x_in.shape[2]
    head_count = decay_log.shape[1]
    head_dim = embedding_width // head_count
    blocks = tok_dev // SPAN
    inner_count = SPAN_BITS + 1
    seq_bits = lax.axis_size("seq").bit_length() - 1
    x_blocks = x_in[0].reshape(blocks, SPAN, head_count, head_dim)
    b_blocks = keys_b[0].reshape(blocks, SPAN, -1)
    c_blocks = queries_c[0].reshape(blocks, SPAN, -1)
    a_blocks = decay_log[0].reshape(head_count, blocks, SPAN)
    mix_all = level_mix[0].reshape(level_mix.shape[1], head_count, blocks, SPAN)
    local_parts, block_states, block_decays, runnings = ([], [], [], [])
    block_index = 0
    local_part, block_state, running = block_inner(
        x_blocks[block_index],
        b_blocks[block_index],
        c_blocks[block_index],
        a_blocks[:, block_index],
        mix_all[:inner_count, :, block_index],
    )
    local_parts.append(local_part)
    block_states.append(block_state)
    block_decays.append(running[:, -1])
    runnings.append(running)
    summary = jnp.zeros_like(block_states[0])
    block_index = 0
    summary = (
        jnp.exp(block_decays[block_index])[:, None, None] * summary + block_states[block_index]
    )
    summary_decay = block_decays[block_index]
    rank_here = lax.axis_index("seq")
    own_prefix = jnp.zeros((head_count,), jnp.float32)
    device_levels = []
    for bit_index in range(seq_bits):
        other_state, other_decay = swapped((summary.astype(jnp.bfloat16), summary_decay), "seq", bit_index)
        other_state = other_state.astype(jnp.float32)
        is_upper = rank_here >> bit_index & 1 == 1
        device_levels.append(
            jnp.where(is_upper, jnp.exp(own_prefix)[:, None, None] * other_state, 0.0)
        )
        lower_state = jnp.where(is_upper, other_state, summary)
        lower_decay = jnp.where(is_upper, other_decay, summary_decay)
        upper_state = jnp.where(is_upper, summary, other_state)
        upper_decay = jnp.where(is_upper, summary_decay, other_decay)
        summary = jnp.exp(upper_decay)[:, None, None] * lower_state + upper_state
        summary_decay = lower_decay + upper_decay
        own_prefix = jnp.where(is_upper, own_prefix + other_decay, own_prefix)
    zero_decay = jnp.zeros((head_count,), jnp.float32)
    block_index = 0
    levels = []
    lead_decay = sum(block_decays[:block_index], zero_decay)
    for device_level in device_levels:
        levels.append(jnp.exp(lead_decay)[:, None, None] * device_level)
    distant = block_distant(
        c_blocks[block_index], runnings[block_index], mix_all[inner_count:, :, block_index], levels
    )
    outputs = local_parts[block_index] + distant
    mixed = outputs.reshape(tok_dev, embedding_width)
    gated = mixed * jax.nn.silu(gate_in[0].astype(jnp.float32))
    normed = (
        gated * lax.rsqrt(jnp.mean(gated * gated, axis=-1, keepdims=True) + EPS) * norm_gain
    ).astype(jnp.bfloat16)
    return gathered_projection(normed, w_gate, w_up)[None]


def solution(mesh):
    in_specs = (
        P("dp", "seq", None),
        P("dp", "seq", None),
        P("dp", "seq", None),
        P("dp", "seq", None),
        P("dp", None, "seq"),
        P("dp", None, None, "seq"),
        P(),
        P(None, ("seq", "dp")),
        P(None, ("seq", "dp")),
    )
    out_specs = P("dp", "seq", None)
    return jax.shard_map(
        per_device, mesh=mesh, in_specs=in_specs, out_specs=out_specs, check_vma=False
    )
```

```python
import jax
import jax.numpy as jnp
from jax import lax
from jax.experimental import pallas as pl
from jax.experimental.pallas import tpu as pltpu
from jax.sharding import PartitionSpec as P

SPAN = 256
SPAN_BITS = 8


EPS = 1e-05
HIGH = lax.Precision.HIGHEST


def swapped(value, axis, distance):
    mask = 2**distance
    pairs = [(source, source ^ mask) for source in range(lax.axis_size(axis))]
    return lax.ppermute(value, axis, pairs)


def top_bit(values):
    powers = jnp.arange(1, 31, dtype=jnp.int32)
    return jnp.sum(values[..., None] >> powers > 0, axis=-1)


def block_inner(x_blk, b_blk, c_blk, a_blk, mix_low):
    length = a_blk.shape[1]
    inner_count = mix_low.shape[0]
    running = jnp.cumsum(a_blk, axis=1)
    position = jnp.arange(length, dtype=jnp.int32)
    differ = position[:, None] ^ position[None, :]
    level_table = jnp.where(differ > 0, top_bit(differ) + 1, 0)
    level_picks = (
        level_table[None] == jnp.arange(inner_count, dtype=jnp.int32)[:, None, None]
    ).astype(jnp.float32)
    chosen = jnp.einsum("lht,lts->hts", mix_low, level_picks, precision=HIGH)
    causal_mask = position[:, None] >= position[None, :]
    log_gap = jnp.where(causal_mask[None], running[:, :, None] - running[:, None, :], -jnp.inf)
    scores = jnp.dot(c_blk, b_blk.T, preferred_element_type=jnp.float32)
    weights = (chosen * jnp.exp(log_gap) * scores[None]).astype(jnp.bfloat16)
    local_part = jnp.einsum("hts,shp->thp", weights, x_blk, preferred_element_type=jnp.float32)
    tail_decay = jnp.exp(running[:, -1:] - running)
    scaled_keys = (tail_decay.T[:, :, None] * b_blk[:, None, :]).astype(jnp.bfloat16)
    block_state = jnp.einsum("shn,shp->hnp", scaled_keys, x_blk, preferred_element_type=jnp.float32)
    return (local_part, block_state, running)


def block_distant(c_blk, running, mix_high, levels):
    growth = jnp.exp(running)
    distant_sum = jnp.zeros((c_blk.shape[0], running.shape[0], levels[0].shape[2]), jnp.float32)
    for level_rank in range(len(levels)):
        level_scale = (mix_high[level_rank] * growth).T
        product = jnp.einsum(
            "tn,hnp->thp",
            c_blk,
            levels[level_rank].astype(jnp.bfloat16),
            preferred_element_type=jnp.float32,
        )
        distant_sum = distant_sum + level_scale[:, :, None] * product
    return distant_sum


def gathered_projection(normed, w_gate, w_up):
    tok_dev = normed.shape[0]
    paired = jnp.stack([w_gate, w_up])
    dp_count = lax.axis_size("dp")
    seq_count = lax.axis_size("seq")
    seq_weights = lax.all_gather(paired, "seq", axis=2, tiled=True)
    projected = jnp.einsum(
        "td,gdk->gtk",
        normed,
        lax.all_gather(seq_weights, "dp", axis=2, tiled=True),
        preferred_element_type=jnp.float32,
    )
    returned = (jax.nn.silu(projected[0]) * projected[1]).astype(jnp.bfloat16)
    hidden = (
        returned.reshape(tok_dev, dp_count, seq_count, -1)
        .transpose(0, 2, 1, 3)
        .reshape(tok_dev, -1)
    )
    return hidden


MESH = pl.DeviceIdType.MESH
SEQ_COUNT = 8
DP_COUNT = 4
LINE = 4
CHIPS = 16
PARTS = 3


def line_member(z, steps):
    place = z + (z >= 2) * (5 - 2 * z)
    back = lax.rem(place - steps + 2 * LINE, LINE)
    return back + (back >= 2) * (5 - 2 * back)


class Gather:
    def __init__(self, piece, held, z_sems, x_sems, y_sems, core_sems, own_sem):
        self.piece, self.held, self.own_sem = piece, held, own_sem
        self.sems = {"z": z_sems, "x": x_sems, "y": y_sems, "core": core_sems}
        seq, dp = lax.axis_index("seq"), lax.axis_index("dp")
        self.seq, self.dp = seq, dp
        self.z, self.x, self.y, self.core = seq // 2, lax.rem(seq, 2), dp // 2, lax.rem(dp, 2)
        self.targets = {
            "z": (line_member(self.z, -1) * 2 + self.x, dp),
            "x": (self.z * 2 + 1 - self.x, dp),
            "y": (seq, (1 - self.y) * 2 + self.core),
            "core": (seq, self.y * 2 + 1 - self.core),
        }
        self.before = (line_member(self.z, 1) * 2 + self.x, dp)
        rows = piece.shape[0]
        side = (rows // 3 + 15) // 16 * 16
        self.cuts = ((0, side), (side, rows - 2 * side), (rows - side, side))
        self.sent = []

    def greet(self):
        barrier = pltpu.get_barrier_semaphore()
        others = list(self.targets.values()) + [self.before]
        for other in others:
            pl.semaphore_signal(barrier, inc=1, device_id=other, device_id_type=MESH)
        pl.semaphore_wait(barrier, len(others))

    def chip(self, step, flip_x, flip_y):
        x = 1 - self.x if flip_x else self.x
        y = 1 - self.y if flip_y else self.y
        return line_member(self.z, step) * 4 + x * 2 + y

    def copy(self, way, slot, chip, part, own=False):
        first, count = self.cuts[part]
        place = self.held.at[chip, self.core, pl.ds(first, count)]
        return pltpu.make_async_remote_copy(
            src_ref=self.piece.at[pl.ds(first, count)] if own else place,
            dst_ref=place,
            send_sem=self.sems[way].at[0, slot],
            recv_sem=self.sems[way].at[1, slot],
            device_id=self.targets[way],
            device_id_type=MESH,
        )

    def send(self, way, slot, chip, part, own=False):
        copy = self.copy(way, slot, chip, part, own)
        copy.start()
        self.sent.append(copy)

    def start(self):
        chip = self.chip(0, 0, 0)
        self.own = pltpu.make_async_copy(self.piece, self.held.at[chip, self.core], self.own_sem)
        self.own.start()
        for part in range(PARTS):
            for way in ("z", "y"):
                self.send(way, part, chip, part, own=True)
        self.send("x", 0, chip, 0, own=True)

    def start_rest(self):
        chip = self.chip(0, 0, 0)
        for part in range(1, PARTS):
            self.send("x", part, chip, part, own=True)
        for part in range(PARTS):
            self.send("core", part, chip, part, own=True)

    def line(self, step, part):
        chip = self.chip(step, 0, 0)
        self.copy("z", (step - 1) * PARTS + part, chip, part).wait_recv()
        if step < LINE - 1:
            self.send("z", step * PARTS + part, chip, part)
        for way in ("x", "y"):
            self.send(way, step * PARTS + part, chip, part)
        self.send("core", step * 4 * PARTS + part, chip, part)

    def across_x(self, step, part):
        chip = self.chip(step, 1, 0)
        self.copy("x", step * PARTS + part, chip, part).wait_recv()
        if part == 0:
            self.send("y", PARTS * LINE + step, chip, part)
        if part == 2 and step == 0:
            self.send("y", (PARTS + 1) * LINE, chip, part)
        self.send("core", (step * 4 + 1) * PARTS + part, chip, part)

    def across_y(self, step, part):
        chip = self.chip(step, 0, 1)
        self.copy("y", step * PARTS + part, chip, part).wait_recv()
        if part == 1:
            self.send("x", PARTS * LINE + step, chip, part)
        self.send("core", (step * 4 + 2) * PARTS + part, chip, part)

    def across(self, step, part):
        self.across_x(step, part)
        self.across_y(step, part)

    def corner(self, step):
        chip = self.chip(step, 1, 1)
        for part, way in enumerate(("y", "x")):
            self.copy(way, PARTS * LINE + step, chip, part).wait_recv()
            self.send("core", (step * 4 + 3) * PARTS + part, chip, part)

    def corner_line(self, step):
        chip, part = self.chip(step, 1, 1), 2
        if step:
            way, slot = "z", PARTS * (LINE - 1) + step - 1
        else:
            way, slot = "y", (PARTS + 1) * LINE
        self.copy(way, slot, chip, part).wait_recv()
        if step < LINE - 1:
            self.send("z", PARTS * (LINE - 1) + step, chip, part)
        self.send("core", (step * 4 + 3) * PARTS + part, chip, part)

    def ready(self, step, kind):
        chip = self.chip(step, kind % 2, kind // 2)
        for part in range(PARTS):
            first, count = self.cuts[part]
            place = self.held.at[chip, 1 - self.core, pl.ds(first, count)]
            slot = (step * 4 + kind) * PARTS + part
            pltpu.make_async_remote_copy(
                src_ref=place,
                dst_ref=place,
                send_sem=self.sems["core"].at[0, slot],
                recv_sem=self.sems["core"].at[1, slot],
                device_id=self.targets["core"],
                device_id_type=MESH,
            ).wait_recv()
        return chip

    def finish(self):
        for copy in self.sent:
            copy.wait_send()


NT = (((1,), (1,)), ((), ()))
HALF = SPAN // 2
GROUP = 4


def rows_of(index, count):
    return pl.ds(pl.multiple_of(index * count, count), count)


def layer_kernel(
    x_in, gate_in, keys, queries, decay, mix, gain, piece, hidden,
    held, x_cols, gate_cols, gain_cols, normed, mixed, run_col, run_row, tail, level_scale,
    level_of, scores, state, state_out, state_in, decay_out, decay_in,
    z_sems, x_sems, y_sems, core_sems, own_sem, state_sems, decay_sems,
):
    gather = Gather(piece, held, z_sems, x_sems, y_sems, core_sems, own_sem)
    gather.greet()
    gather.start()
    heads = decay.shape[0]
    head_dim = x_cols.shape[0] // heads
    seq, dp = gather.seq, gather.dp
    f32, bf16 = jnp.float32, jnp.bfloat16

    def exchange(bit):
        target = (seq + (1 - 2 * (seq // 2**bit % 2)) * 2**bit, dp)
        pairs = [(state_out, state_in, state_sems), (decay_out, decay_in, decay_sems)]
        return [
            pltpu.make_async_remote_copy(
                src_ref=source.at[bit],
                dst_ref=place.at[bit],
                send_sem=sems.at[0, bit],
                recv_sem=sems.at[1, bit],
                device_id=target,
                device_id_type=MESH,
            )
            for source, place, sems in pairs[: 1 if bit == 2 else 2]
        ]

    before = lax.broadcasted_iota(jnp.int32, (SPAN, SPAN), 0)
    after = lax.broadcasted_iota(jnp.int32, (SPAN, SPAN), 1)
    up_to = (before <= after).astype(f32)
    run = jnp.dot(decay[...], up_to, precision=HIGH, preferred_element_type=f32)
    run_row[...] = run
    tail[...] = jnp.exp(jnp.minimum(run[:, SPAN - 1 :] - run, 0.0))
    total = jnp.broadcast_to(run[:, SPAN - 1 :], (heads, 128))
    decay_out[0] = total

    def turn(index, _):
        lanes = rows_of(index, 128)
        x_cols[lanes, :] = x_in[:, lanes].astype(f32).T.astype(bf16)
        return 0

    lax.fori_loop(0, x_cols.shape[0] // 128, turn, 0)

    def block_states(index, _):
        parts = []
        for place in range(GROUP):
            head = index * GROUP + place
            values = x_cols[rows_of(head, head_dim), :].astype(f32) * tail[pl.ds(head, 1), :]
            parts.append(values.astype(bf16))
        rows = rows_of(index, GROUP * head_dim)
        result = jnp.dot(jnp.concatenate(parts), keys[...], preferred_element_type=f32)
        state[rows, :] = result
        state_out[0, rows, :] = result.astype(bf16)
        return 0

    lax.fori_loop(0, heads // GROUP, block_states, 0)
    rounds = [exchange(0)]
    for copy in rounds[0]:
        copy.start()
    gather.start_rest()

    gather.line(1, 0)
    gather.across(0, 0)

    columns = lax.dot_general(
        (before >= after).astype(f32), decay[...], NT, precision=HIGH, preferred_element_type=f32
    )
    for head in range(heads):
        run_col[head] = jnp.broadcast_to(columns[:, head : head + 1], (SPAN, 128))
    scores[...] = lax.dot_general(keys[...], queries[...], NT, preferred_element_type=f32)
    source = lax.broadcasted_iota(jnp.int32, (HALF, HALF), 0)
    target = lax.broadcasted_iota(jnp.int32, (HALF, HALF), 1)
    differ = source ^ target
    level = jnp.zeros((HALF, HALF), jnp.int32)
    for bit in range(SPAN_BITS - 1):
        level = level + (differ >= 2**bit).astype(jnp.int32)
    level_of[...] = jnp.where(source <= target, level, -1)

    gather.line(1, 1)
    gather.across(0, 1)
    gather.line(1, 2)
    gather.across(0, 2)

    def local(head, _):
        run_t = run_row[pl.ds(head, 1), :]
        mixes = [mix[rank, pl.ds(head, 1), :] for rank in range(SPAN_BITS + 1)]
        values = x_cols[rows_of(head, head_dim), :]
        weights = []
        for first in (0, HALF):
            span = slice(first, first + HALF)
            gap = run_t[:, span] - run_col[head, span, :]
            levels = level_of[...]
            chosen = jnp.zeros((HALF, HALF), f32)
            for rank in range(SPAN_BITS):
                chosen = jnp.where(levels == rank, mixes[rank][:, span], chosen)
            weights.append(chosen * jnp.exp(jnp.minimum(gap, 0.0)) * scores[span, span])
        gap = run_t[:, HALF:] - run_col[head, :HALF, :]
        cross = mixes[SPAN_BITS][:, HALF:] * jnp.exp(jnp.minimum(gap, 0.0))
        cross = (cross * scores[:HALF, HALF:]).astype(bf16)
        rows = rows_of(head, head_dim)
        mixed[rows, :HALF] = jnp.dot(
            values[:, :HALF], weights[0].astype(bf16), preferred_element_type=f32
        )
        mixed[rows, HALF:] = jnp.dot(
            values, jnp.concatenate([cross, weights[1].astype(bf16)]), preferred_element_type=f32
        )
        return 0

    def locals_of(quarter):
        lax.fori_loop(quarter * heads // 4, (quarter + 1) * heads // 4, local, 0)

    prefix = jnp.zeros((heads, 128), f32)

    def scale_level(bit, prefix):
        upper = (seq // 2**bit % 2).astype(f32)
        growth = jnp.exp(run_row[...] + jnp.concatenate([prefix] * 2, axis=1))
        level_scale[bit] = upper * mix[SPAN_BITS + 1 + bit] * growth

    def merge(bit, total, prefix):
        for copy in rounds[bit]:
            copy.wait_recv()
        other = decay_in[bit]
        upper = (seq // 2**bit % 2).astype(f32)
        scale_level(bit, prefix)
        tail[:, :128] = jnp.exp((1.0 - upper) * other)
        tail[:, 128:] = jnp.exp(upper * total)

        def add(head, _):
            rows = rows_of(head, head_dim)
            factors = tail[pl.ds(head, 1), :]
            mine = factors[:, :128] * state[rows, :]
            both = mine + factors[:, 128:] * state_in[bit, rows, :].astype(f32)
            state[rows, :] = both
            state_out[bit + 1, rows, :] = both.astype(bf16)
            return 0

        lax.fori_loop(0, heads, add, 0)
        total = total + other
        if bit == 0:
            decay_out[1] = total
        rounds.append(exchange(bit + 1))
        for copy in rounds[bit + 1]:
            copy.start()
        return total, prefix + upper * other

    def distant(bit):
        def add(index, _):
            rows = rows_of(index, GROUP * head_dim)
            product = lax.dot_general(
                state_in[bit, rows, :], queries[...], NT, preferred_element_type=f32
            )
            for place in range(GROUP):
                head = index * GROUP + place
                part = product[place * head_dim : (place + 1) * head_dim]
                mixed[rows_of(head, head_dim), :] += level_scale[bit, pl.ds(head, 1), :] * part
            return 0

        lax.fori_loop(0, heads // GROUP, add, 0)

    def turn_gate(index, _):
        lanes = rows_of(index, 128)
        gate_cols[lanes, :] = gate_in[:, lanes].astype(f32).T.astype(bf16)
        gain_cols[lanes, :] = jnp.broadcast_to(gain[:, lanes], (128, 128)).T
        return 0

    lax.fori_loop(0, gate_cols.shape[0] // 128, turn_gate, 0)
    total, prefix = merge(0, total, prefix)
    locals_of(0)
    gather.line(2, 0)
    gather.across(1, 0)
    locals_of(1)
    gather.line(2, 1)
    gather.line(2, 2)
    gather.across(1, 1)
    gather.across(1, 2)
    total, prefix = merge(1, total, prefix)
    scale_level(2, prefix)
    gather.line(3, 0)
    gather.line(3, 1)
    gather.line(3, 2)
    locals_of(2)
    gather.corner(0)
    gather.across(2, 0)
    locals_of(3)
    gather.across(2, 1)
    distant(0)
    gather.across(2, 2)
    distant(1)
    gather.corner(1)
    gather.across(3, 0)
    gather.across(3, 1)
    gather.across(3, 2)
    gather.corner_line(0)
    rounds[2][0].wait_recv()
    distant(2)
    gather.corner_line(1)

    def gated(index, squares):
        rows = rows_of(index, head_dim)
        gate = gate_cols[rows, :].astype(f32)
        value = mixed[rows, :] * (gate / (1.0 + jnp.exp(-gate)))
        mixed[rows, :] = value
        return squares + jnp.sum(value * value, axis=0, keepdims=True)

    squares = lax.fori_loop(0, heads, gated, jnp.zeros((1, SPAN), f32))
    scale = lax.rsqrt(squares / mixed.shape[0] + EPS)

    gather.corner_line(2)

    def norm(index, _):
        rows = rows_of(index, head_dim)
        gains = gain_cols[rows, :]
        value = mixed[rows, :] * scale * jnp.concatenate([gains, gains], axis=1)
        normed[rows, :] = value.astype(bf16)
        return 0

    lax.fori_loop(0, heads, norm, 0)

    rows = piece.shape[0]

    def project(chip):
        weights = held[chip].reshape(2 * rows, held.shape[3])
        both = jnp.dot(weights, normed[...], preferred_element_type=f32)
        gate, up = both[:rows], both[rows:]
        hidden[chip] = (gate / (1.0 + jnp.exp(-gate)) * up).astype(bf16)

    gather.own.wait()
    for step in range(2):
        for kind in range(4):
            project(gather.ready(step, kind))
    gather.corner(2)
    for kind in range(4):
        project(gather.ready(2, kind))
    for kind in range(3):
        project(gather.ready(3, kind))
    gather.corner_line(3)
    gather.corner(3)
    project(gather.ready(3, 3))
    gather.finish()
    for copies in rounds:
        for copy in copies:
            copy.wait_send()


def chip_rows(w_gate, w_up):
    first = lax.axis_index("dp") % 2 == 0
    gate, up = w_gate.T, w_up.T
    pairs = [(source, source ^ 1) for source in range(DP_COUNT)]
    other = lax.ppermute(jnp.where(first, up, gate), "dp", pairs)
    return jnp.where(first, jnp.concatenate([gate, other]), jnp.concatenate([other, up]))


def streamed_layer(x, gate, keys, queries, decay, mix, norm_gain, w_gate, w_up):
    piece = chip_rows(w_gate, w_up)
    rows, depth = piece.shape
    tokens = x.shape[0]
    heads = decay.shape[0]
    states = keys.shape[1]
    sems = pltpu.SemaphoreType.DMA
    f32, bf16 = jnp.float32, jnp.bfloat16
    hidden = pl.pallas_call(
        layer_kernel,
        out_shape=jax.ShapeDtypeStruct((CHIPS, rows, tokens), bf16),
        in_specs=[pl.BlockSpec(memory_space=pltpu.VMEM)] * 8,
        out_specs=pl.BlockSpec(memory_space=pltpu.VMEM),
        scratch_shapes=[
            pltpu.VMEM((CHIPS, 2, rows, depth), bf16),
            pltpu.VMEM((depth, tokens), bf16),
            pltpu.VMEM((depth, tokens), bf16),
            pltpu.VMEM((depth, 128), f32),
            pltpu.VMEM((depth, tokens), bf16),
            pltpu.VMEM((depth, tokens), f32),
            pltpu.VMEM((heads, tokens, 128), f32),
            pltpu.VMEM((heads, tokens), f32),
            pltpu.VMEM((heads, tokens), f32),
            pltpu.VMEM((3, heads, tokens), f32),
            pltpu.VMEM((HALF, HALF), jnp.int32),
            pltpu.VMEM((SPAN, SPAN), f32),
            pltpu.VMEM((depth, states), f32),
            pltpu.VMEM((3, depth, states), bf16),
            pltpu.VMEM((3, depth, states), bf16),
            pltpu.VMEM((2, heads, 128), f32),
            pltpu.VMEM((2, heads, 128), f32),
            sems((2, (PARTS + 1) * (LINE - 1))),
            sems((2, (PARTS + 1) * LINE)),
            sems((2, (PARTS + 1) * LINE + 1)),
            sems((2, PARTS * CHIPS)),
            sems,
            sems((2, 3)),
            sems((2, 2)),
        ],
        compiler_params=pltpu.CompilerParams(
            collective_id=0, has_side_effects=True, vmem_limit_bytes=56 * 2**20
        ),
        cost_estimate=pl.CostEstimate(
            flops=4 * tokens * CHIPS * rows * depth,
            bytes_accessed=2 * CHIPS * rows * depth * 2,
            transcendentals=tokens * CHIPS * rows,
        ),
    )(x, gate, keys, queries, decay, mix, norm_gain[None, :], piece)
    return hidden.reshape(CHIPS * rows, tokens).T


def per_device(x_in, gate_in, keys_b, queries_c, decay_log, level_mix, norm_gain, w_gate, w_up):
    mesh_sizes = (lax.axis_size("seq"), lax.axis_size("dp"))
    if mesh_sizes == (SEQ_COUNT, DP_COUNT) and x_in.shape[1] == SPAN:
        local = (x_in, gate_in, keys_b, queries_c, decay_log, level_mix)
        layer = streamed_layer(*(array[0] for array in local), norm_gain, w_gate, w_up)
        return layer[None]
    tok_dev = x_in.shape[1]
    embedding_width = x_in.shape[2]
    head_count = decay_log.shape[1]
    head_dim = embedding_width // head_count
    blocks = tok_dev // SPAN
    inner_count = SPAN_BITS + 1
    seq_bits = lax.axis_size("seq").bit_length() - 1
    x_blocks = x_in[0].reshape(blocks, SPAN, head_count, head_dim)
    b_blocks = keys_b[0].reshape(blocks, SPAN, -1)
    c_blocks = queries_c[0].reshape(blocks, SPAN, -1)
    a_blocks = decay_log[0].reshape(head_count, blocks, SPAN)
    mix_all = level_mix[0].reshape(level_mix.shape[1], head_count, blocks, SPAN)
    local_parts, block_states, block_decays, runnings = ([], [], [], [])
    block_index = 0
    local_part, block_state, running = block_inner(
        x_blocks[block_index],
        b_blocks[block_index],
        c_blocks[block_index],
        a_blocks[:, block_index],
        mix_all[:inner_count, :, block_index],
    )
    local_parts.append(local_part)
    block_states.append(block_state)
    block_decays.append(running[:, -1])
    runnings.append(running)
    summary = jnp.zeros_like(block_states[0])
    block_index = 0
    summary = (
        jnp.exp(block_decays[block_index])[:, None, None] * summary + block_states[block_index]
    )
    summary_decay = block_decays[block_index]
    rank_here = lax.axis_index("seq")
    own_prefix = jnp.zeros((head_count,), jnp.float32)
    device_levels = []
    for bit_index in range(seq_bits):
        other_state, other_decay = swapped((summary.astype(jnp.bfloat16), summary_decay), "seq", bit_index)
        other_state = other_state.astype(jnp.float32)
        is_upper = rank_here >> bit_index & 1 == 1
        device_levels.append(
            jnp.where(is_upper, jnp.exp(own_prefix)[:, None, None] * other_state, 0.0)
        )
        lower_state = jnp.where(is_upper, other_state, summary)
        lower_decay = jnp.where(is_upper, other_decay, summary_decay)
        upper_state = jnp.where(is_upper, summary, other_state)
        upper_decay = jnp.where(is_upper, summary_decay, other_decay)
        summary = jnp.exp(upper_decay)[:, None, None] * lower_state + upper_state
        summary_decay = lower_decay + upper_decay
        own_prefix = jnp.where(is_upper, own_prefix + other_decay, own_prefix)
    zero_decay = jnp.zeros((head_count,), jnp.float32)
    block_index = 0
    levels = []
    lead_decay = sum(block_decays[:block_index], zero_decay)
    for device_level in device_levels:
        levels.append(jnp.exp(lead_decay)[:, None, None] * device_level)
    distant = block_distant(
        c_blocks[block_index], runnings[block_index], mix_all[inner_count:, :, block_index], levels
    )
    outputs = local_parts[block_index] + distant
    mixed = outputs.reshape(tok_dev, embedding_width)
    gated = mixed * jax.nn.silu(gate_in[0].astype(jnp.float32))
    normed = (
        gated * lax.rsqrt(jnp.mean(gated * gated, axis=-1, keepdims=True) + EPS) * norm_gain
    ).astype(jnp.bfloat16)
    return gathered_projection(normed, w_gate, w_up)[None]


def solution(mesh):
    in_specs = (
        P("dp", "seq", None),
        P("dp", "seq", None),
        P("dp", "seq", None),
        P("dp", "seq", None),
        P("dp", None, "seq"),
        P("dp", None, None, "seq"),
        P(),
        P(None, ("seq", "dp")),
        P(None, ("seq", "dp")),
    )
    out_specs = P("dp", "seq", None)
    return jax.shard_map(
        per_device, mesh=mesh, in_specs=in_specs, out_specs=out_specs, check_vma=False
    )
```

```python
import jax
import jax.numpy as jnp
from jax import lax
from jax.experimental import pallas as pl
from jax.experimental.pallas import tpu as pltpu
from jax.sharding import PartitionSpec as P

SPAN = 256
SPAN_BITS = 8


EPS = 1e-05
HIGH = lax.Precision.HIGHEST


def swapped(value, axis, distance):
    mask = 2**distance
    pairs = [(source, source ^ mask) for source in range(lax.axis_size(axis))]
    return lax.ppermute(value, axis, pairs)


def top_bit(values):
    powers = jnp.arange(1, 31, dtype=jnp.int32)
    return jnp.sum(values[..., None] >> powers > 0, axis=-1)


def block_inner(x_blk, b_blk, c_blk, a_blk, mix_low):
    length = a_blk.shape[1]
    inner_count = mix_low.shape[0]
    running = jnp.cumsum(a_blk, axis=1)
    position = jnp.arange(length, dtype=jnp.int32)
    differ = position[:, None] ^ position[None, :]
    level_table = jnp.where(differ > 0, top_bit(differ) + 1, 0)
    level_picks = (
        level_table[None] == jnp.arange(inner_count, dtype=jnp.int32)[:, None, None]
    ).astype(jnp.float32)
    chosen = jnp.einsum("lht,lts->hts", mix_low, level_picks, precision=HIGH)
    causal_mask = position[:, None] >= position[None, :]
    log_gap = jnp.where(causal_mask[None], running[:, :, None] - running[:, None, :], -jnp.inf)
    scores = jnp.dot(c_blk, b_blk.T, preferred_element_type=jnp.float32)
    weights = (chosen * jnp.exp(log_gap) * scores[None]).astype(jnp.bfloat16)
    local_part = jnp.einsum("hts,shp->thp", weights, x_blk, preferred_element_type=jnp.float32)
    tail_decay = jnp.exp(running[:, -1:] - running)
    scaled_keys = (tail_decay.T[:, :, None] * b_blk[:, None, :]).astype(jnp.bfloat16)
    block_state = jnp.einsum("shn,shp->hnp", scaled_keys, x_blk, preferred_element_type=jnp.float32)
    return (local_part, block_state, running)


def block_distant(c_blk, running, mix_high, levels):
    growth = jnp.exp(running)
    distant_sum = jnp.zeros((c_blk.shape[0], running.shape[0], levels[0].shape[2]), jnp.float32)
    for level_rank in range(len(levels)):
        level_scale = (mix_high[level_rank] * growth).T
        product = jnp.einsum(
            "tn,hnp->thp",
            c_blk,
            levels[level_rank].astype(jnp.bfloat16),
            preferred_element_type=jnp.float32,
        )
        distant_sum = distant_sum + level_scale[:, :, None] * product
    return distant_sum


def gathered_projection(normed, w_gate, w_up):
    tok_dev = normed.shape[0]
    paired = jnp.stack([w_gate, w_up])
    dp_count = lax.axis_size("dp")
    seq_count = lax.axis_size("seq")
    seq_weights = lax.all_gather(paired, "seq", axis=2, tiled=True)
    projected = jnp.einsum(
        "td,gdk->gtk",
        normed,
        lax.all_gather(seq_weights, "dp", axis=2, tiled=True),
        preferred_element_type=jnp.float32,
    )
    returned = (jax.nn.silu(projected[0]) * projected[1]).astype(jnp.bfloat16)
    hidden = (
        returned.reshape(tok_dev, dp_count, seq_count, -1)
        .transpose(0, 2, 1, 3)
        .reshape(tok_dev, -1)
    )
    return hidden


MESH = pl.DeviceIdType.MESH
SEQ_COUNT = 8
DP_COUNT = 4
LINE = 4
CHIPS = 16


def line_member(z, steps):
    place = z + (z >= 2) * (5 - 2 * z)
    back = lax.rem(place - steps + 2 * LINE, LINE)
    return back + (back >= 2) * (5 - 2 * back)


class Gather:
    def __init__(self, piece, held, z_sems, x_sems, y_sems, core_sems, own_sem):
        self.piece, self.held, self.own_sem = piece, held, own_sem
        self.sems = {"z": z_sems, "x": x_sems, "y": y_sems, "core": core_sems}
        seq, dp = lax.axis_index("seq"), lax.axis_index("dp")
        self.seq, self.dp = seq, dp
        self.z, self.x, self.y, self.core = seq // 2, lax.rem(seq, 2), dp // 2, lax.rem(dp, 2)
        self.targets = {
            "z": (line_member(self.z, -1) * 2 + self.x, dp),
            "x": (self.z * 2 + 1 - self.x, dp),
            "y": (seq, (1 - self.y) * 2 + self.core),
            "core": (seq, self.y * 2 + 1 - self.core),
        }
        self.before = (line_member(self.z, 1) * 2 + self.x, dp)
        rows = piece.shape[0]
        cut = (rows // 2 + 15) // 16 * 16
        self.cuts = ((0, cut), (cut, rows - cut))
        self.sent = []

    def greet(self):
        barrier = pltpu.get_barrier_semaphore()
        others = list(self.targets.values()) + [self.before]
        for other in others:
            pl.semaphore_signal(barrier, inc=1, device_id=other, device_id_type=MESH)
        pl.semaphore_wait(barrier, len(others))

    def chip(self, step, flip_x, flip_y):
        x = 1 - self.x if flip_x else self.x
        y = 1 - self.y if flip_y else self.y
        return line_member(self.z, step) * 4 + x * 2 + y

    def copy(self, way, slot, chip, part, own=False):
        first, count = self.cuts[part]
        place = self.held.at[chip, self.core, pl.ds(first, count)]
        return pltpu.make_async_remote_copy(
            src_ref=self.piece.at[pl.ds(first, count)] if own else place,
            dst_ref=place,
            send_sem=self.sems[way].at[0, slot],
            recv_sem=self.sems[way].at[1, slot],
            device_id=self.targets[way],
            device_id_type=MESH,
        )

    def send(self, way, slot, chip, part, own=False):
        copy = self.copy(way, slot, chip, part, own)
        copy.start()
        self.sent.append(copy)

    def start(self):
        chip = self.chip(0, 0, 0)
        self.own = pltpu.make_async_copy(self.piece, self.held.at[chip, self.core], self.own_sem)
        self.own.start()
        for part in range(2):
            for way in ("z", "y"):
                self.send(way, part, chip, part, own=True)
        self.send("x", 0, chip, 0, own=True)

    def start_rest(self):
        chip = self.chip(0, 0, 0)
        self.send("x", 1, chip, 1, own=True)
        for part in range(2):
            self.send("core", part, chip, part, own=True)

    def line(self, step, part):
        chip = self.chip(step, 0, 0)
        self.copy("z", (step - 1) * 2 + part, chip, part).wait_recv()
        if step < LINE - 1:
            self.send("z", step * 2 + part, chip, part)
        for way in ("x", "y"):
            self.send(way, step * 2 + part, chip, part)
        self.send("core", step * 8 + part, chip, part)

    def across_x(self, step, part):
        chip = self.chip(step, 1, 0)
        self.copy("x", step * 2 + part, chip, part).wait_recv()
        if part == 0:
            self.send("y", 2 * LINE + step, chip, part)
        self.send("core", step * 8 + 2 + part, chip, part)

    def across_y(self, step, part):
        chip = self.chip(step, 0, 1)
        self.copy("y", step * 2 + part, chip, part).wait_recv()
        if part == 1:
            self.send("x", 2 * LINE + step, chip, part)
        self.send("core", step * 8 + 4 + part, chip, part)

    def across(self, step, part):
        self.across_x(step, part)
        self.across_y(step, part)

    def corner(self, step):
        chip = self.chip(step, 1, 1)
        for part, way in enumerate(("y", "x")):
            self.copy(way, 2 * LINE + step, chip, part).wait_recv()
            self.send("core", step * 8 + 6 + part, chip, part)

    def ready(self, step, kind):
        chip = self.chip(step, kind % 2, kind // 2)
        for part in range(2):
            first, count = self.cuts[part]
            place = self.held.at[chip, 1 - self.core, pl.ds(first, count)]
            slot = step * 8 + kind * 2 + part
            pltpu.make_async_remote_copy(
                src_ref=place,
                dst_ref=place,
                send_sem=self.sems["core"].at[0, slot],
                recv_sem=self.sems["core"].at[1, slot],
                device_id=self.targets["core"],
                device_id_type=MESH,
            ).wait_recv()
        return chip

    def finish(self):
        for copy in self.sent:
            copy.wait_send()


NT = (((1,), (1,)), ((), ()))
HALF = SPAN // 2
GROUP = 4


def rows_of(index, count):
    return pl.ds(pl.multiple_of(index * count, count), count)


def layer_kernel(
    x_in, gate_in, keys, queries, decay, mix, gain, piece, hidden,
    held, x_cols, gate_cols, gain_cols, normed, mixed, run_col, run_row, tail, level_scale,
    level_of, scores, state, state_out, state_in, decay_out, decay_in,
    z_sems, x_sems, y_sems, core_sems, own_sem, state_sems, decay_sems,
):
    gather = Gather(piece, held, z_sems, x_sems, y_sems, core_sems, own_sem)
    gather.greet()
    gather.start()
    heads = decay.shape[0]
    head_dim = x_cols.shape[0] // heads
    seq, dp = gather.seq, gather.dp
    f32, bf16 = jnp.float32, jnp.bfloat16

    def exchange(bit):
        target = (seq + (1 - 2 * (seq // 2**bit % 2)) * 2**bit, dp)
        pairs = [(state_out, state_in, state_sems), (decay_out, decay_in, decay_sems)]
        return [
            pltpu.make_async_remote_copy(
                src_ref=source.at[bit],
                dst_ref=place.at[bit],
                send_sem=sems.at[0, bit],
                recv_sem=sems.at[1, bit],
                device_id=target,
                device_id_type=MESH,
            )
            for source, place, sems in pairs[: 1 if bit == 2 else 2]
        ]

    before = lax.broadcasted_iota(jnp.int32, (SPAN, SPAN), 0)
    after = lax.broadcasted_iota(jnp.int32, (SPAN, SPAN), 1)
    up_to = (before <= after).astype(f32)
    run = jnp.dot(decay[...], up_to, precision=HIGH, preferred_element_type=f32)
    run_row[...] = run
    tail[...] = jnp.exp(jnp.minimum(run[:, SPAN - 1 :] - run, 0.0))
    total = jnp.broadcast_to(run[:, SPAN - 1 :], (heads, 128))
    decay_out[0] = total

    def turn(index, _):
        lanes = rows_of(index, 128)
        x_cols[lanes, :] = x_in[:, lanes].astype(f32).T.astype(bf16)
        return 0

    lax.fori_loop(0, x_cols.shape[0] // 128, turn, 0)

    def block_states(index, _):
        parts = []
        for place in range(GROUP):
            head = index * GROUP + place
            values = x_cols[rows_of(head, head_dim), :].astype(f32) * tail[pl.ds(head, 1), :]
            parts.append(values.astype(bf16))
        rows = rows_of(index, GROUP * head_dim)
        result = jnp.dot(jnp.concatenate(parts), keys[...], preferred_element_type=f32)
        state[rows, :] = result
        state_out[0, rows, :] = result.astype(bf16)
        return 0

    lax.fori_loop(0, heads // GROUP, block_states, 0)
    rounds = [exchange(0)]
    for copy in rounds[0]:
        copy.start()
    gather.start_rest()

    gather.line(1, 0)
    gather.across(0, 0)

    columns = lax.dot_general(
        (before >= after).astype(f32), decay[...], NT, precision=HIGH, preferred_element_type=f32
    )
    for head in range(heads):
        run_col[head] = jnp.broadcast_to(columns[:, head : head + 1], (SPAN, 128))
    scores[...] = lax.dot_general(keys[...], queries[...], NT, preferred_element_type=f32)
    source = lax.broadcasted_iota(jnp.int32, (HALF, HALF), 0)
    target = lax.broadcasted_iota(jnp.int32, (HALF, HALF), 1)
    differ = source ^ target
    level = jnp.zeros((HALF, HALF), jnp.int32)
    for bit in range(SPAN_BITS - 1):
        level = level + (differ >= 2**bit).astype(jnp.int32)
    level_of[...] = jnp.where(source <= target, level, -1)

    gather.line(1, 1)
    gather.across(0, 1)

    def local(head, _):
        run_t = run_row[pl.ds(head, 1), :]
        mixes = [mix[rank, pl.ds(head, 1), :] for rank in range(SPAN_BITS + 1)]
        values = x_cols[rows_of(head, head_dim), :]
        weights = []
        for first in (0, HALF):
            span = slice(first, first + HALF)
            gap = run_t[:, span] - run_col[head, span, :]
            levels = level_of[...]
            chosen = jnp.zeros((HALF, HALF), f32)
            for rank in range(SPAN_BITS):
                chosen = jnp.where(levels == rank, mixes[rank][:, span], chosen)
            weights.append(chosen * jnp.exp(jnp.minimum(gap, 0.0)) * scores[span, span])
        gap = run_t[:, HALF:] - run_col[head, :HALF, :]
        cross = mixes[SPAN_BITS][:, HALF:] * jnp.exp(jnp.minimum(gap, 0.0))
        cross = (cross * scores[:HALF, HALF:]).astype(bf16)
        rows = rows_of(head, head_dim)
        mixed[rows, :HALF] = jnp.dot(
            values[:, :HALF], weights[0].astype(bf16), preferred_element_type=f32
        )
        mixed[rows, HALF:] = jnp.dot(
            values, jnp.concatenate([cross, weights[1].astype(bf16)]), preferred_element_type=f32
        )
        return 0

    def locals_of(quarter):
        lax.fori_loop(quarter * heads // 4, (quarter + 1) * heads // 4, local, 0)

    prefix = jnp.zeros((heads, 128), f32)

    def scale_level(bit, prefix):
        upper = (seq // 2**bit % 2).astype(f32)
        growth = jnp.exp(run_row[...] + jnp.concatenate([prefix] * 2, axis=1))
        level_scale[bit] = upper * mix[SPAN_BITS + 1 + bit] * growth

    def merge(bit, total, prefix):
        for copy in rounds[bit]:
            copy.wait_recv()
        other = decay_in[bit]
        upper = (seq // 2**bit % 2).astype(f32)
        scale_level(bit, prefix)
        tail[:, :128] = jnp.exp((1.0 - upper) * other)
        tail[:, 128:] = jnp.exp(upper * total)

        def add(head, _):
            rows = rows_of(head, head_dim)
            factors = tail[pl.ds(head, 1), :]
            mine = factors[:, :128] * state[rows, :]
            both = mine + factors[:, 128:] * state_in[bit, rows, :].astype(f32)
            state[rows, :] = both
            state_out[bit + 1, rows, :] = both.astype(bf16)
            return 0

        lax.fori_loop(0, heads, add, 0)
        total = total + other
        if bit == 0:
            decay_out[1] = total
        rounds.append(exchange(bit + 1))
        for copy in rounds[bit + 1]:
            copy.start()
        return total, prefix + upper * other

    def distant(bit):
        def add(index, _):
            rows = rows_of(index, GROUP * head_dim)
            product = lax.dot_general(
                state_in[bit, rows, :], queries[...], NT, preferred_element_type=f32
            )
            for place in range(GROUP):
                head = index * GROUP + place
                part = product[place * head_dim : (place + 1) * head_dim]
                mixed[rows_of(head, head_dim), :] += level_scale[bit, pl.ds(head, 1), :] * part
            return 0

        lax.fori_loop(0, heads // GROUP, add, 0)

    total, prefix = merge(0, total, prefix)
    locals_of(0)
    gather.line(2, 0)
    gather.across(1, 0)
    locals_of(1)
    gather.line(2, 1)
    gather.across(1, 1)
    total, prefix = merge(1, total, prefix)
    scale_level(2, prefix)
    gather.line(3, 0)
    gather.corner(0)
    locals_of(2)
    gather.line(3, 1)
    gather.across(2, 0)
    locals_of(3)
    distant(0)
    gather.across(2, 1)
    distant(1)
    gather.corner(1)

    def turn_gate(index, _):
        lanes = rows_of(index, 128)
        gate_cols[lanes, :] = gate_in[:, lanes].astype(f32).T.astype(bf16)
        gain_cols[lanes, :] = jnp.broadcast_to(gain[:, lanes], (128, 128)).T
        return 0

    lax.fori_loop(0, gate_cols.shape[0] // 128, turn_gate, 0)
    gather.across(3, 0)
    gather.across(3, 1)
    rounds[2][0].wait_recv()
    distant(2)

    def gated(index, squares):
        rows = rows_of(index, head_dim)
        gate = gate_cols[rows, :].astype(f32)
        value = mixed[rows, :] * (gate / (1.0 + jnp.exp(-gate)))
        mixed[rows, :] = value
        return squares + jnp.sum(value * value, axis=0, keepdims=True)

    squares = lax.fori_loop(0, heads, gated, jnp.zeros((1, SPAN), f32))
    scale = lax.rsqrt(squares / mixed.shape[0] + EPS)

    def norm(index, _):
        rows = rows_of(index, head_dim)
        gains = gain_cols[rows, :]
        value = mixed[rows, :] * scale * jnp.concatenate([gains, gains], axis=1)
        normed[rows, :] = value.astype(bf16)
        return 0

    lax.fori_loop(0, heads, norm, 0)

    rows = piece.shape[0]

    def project_pair(step, kind):
        chip = gather.ready(step, kind) // 2 * 2
        gather.ready(step, kind + 2)
        weights = held[pl.ds(chip, 2)].reshape(4 * rows, held.shape[3])
        both = jnp.dot(weights, normed[...], preferred_element_type=f32)
        both = both.reshape(2, 2, rows, SPAN)
        gate, up = both[:, 0], both[:, 1]
        hidden[pl.ds(chip, 2)] = (gate / (1.0 + jnp.exp(-gate)) * up).astype(bf16)

    gather.own.wait()
    for step in range(2):
        project_pair(step, 0)
        project_pair(step, 1)
    gather.corner(2)
    project_pair(2, 0)
    project_pair(2, 1)
    project_pair(3, 0)
    gather.corner(3)
    project_pair(3, 1)
    gather.finish()
    for copies in rounds:
        for copy in copies:
            copy.wait_send()


def chip_rows(w_gate, w_up):
    first = lax.axis_index("dp") % 2 == 0
    gate, up = w_gate.T, w_up.T
    pairs = [(source, source ^ 1) for source in range(DP_COUNT)]
    other = lax.ppermute(jnp.where(first, up, gate), "dp", pairs)
    return jnp.where(first, jnp.concatenate([gate, other]), jnp.concatenate([other, up]))


def streamed_layer(x, gate, keys, queries, decay, mix, norm_gain, w_gate, w_up):
    piece = chip_rows(w_gate, w_up)
    rows, depth = piece.shape
    tokens = x.shape[0]
    heads = decay.shape[0]
    states = keys.shape[1]
    sems = pltpu.SemaphoreType.DMA
    f32, bf16 = jnp.float32, jnp.bfloat16
    hidden = pl.pallas_call(
        layer_kernel,
        out_shape=jax.ShapeDtypeStruct((CHIPS, rows, tokens), bf16),
        in_specs=[pl.BlockSpec(memory_space=pltpu.VMEM)] * 8,
        out_specs=pl.BlockSpec(memory_space=pltpu.VMEM),
        scratch_shapes=[
            pltpu.VMEM((CHIPS, 2, rows, depth), bf16),
            pltpu.VMEM((depth, tokens), bf16),
            pltpu.VMEM((depth, tokens), bf16),
            pltpu.VMEM((depth, 128), f32),
            pltpu.VMEM((depth, tokens), bf16),
            pltpu.VMEM((depth, tokens), f32),
            pltpu.VMEM((heads, tokens, 128), f32),
            pltpu.VMEM((heads, tokens), f32),
            pltpu.VMEM((heads, tokens), f32),
            pltpu.VMEM((3, heads, tokens), f32),
            pltpu.VMEM((HALF, HALF), jnp.int32),
            pltpu.VMEM((SPAN, SPAN), f32),
            pltpu.VMEM((depth, states), f32),
            pltpu.VMEM((3, depth, states), bf16),
            pltpu.VMEM((3, depth, states), bf16),
            pltpu.VMEM((2, heads, 128), f32),
            pltpu.VMEM((2, heads, 128), f32),
            sems((2, 6)),
            sems((2, 12)),
            sems((2, 12)),
            sems((2, 2 * CHIPS)),
            sems,
            sems((2, 3)),
            sems((2, 2)),
        ],
        compiler_params=pltpu.CompilerParams(
            collective_id=0, has_side_effects=True, vmem_limit_bytes=56 * 2**20
        ),
        cost_estimate=pl.CostEstimate(
            flops=4 * tokens * CHIPS * rows * depth,
            bytes_accessed=2 * CHIPS * rows * depth * 2,
            transcendentals=tokens * CHIPS * rows,
        ),
    )(x, gate, keys, queries, decay, mix, norm_gain[None, :], piece)
    return hidden.reshape(CHIPS * rows, tokens).T


def per_device(x_in, gate_in, keys_b, queries_c, decay_log, level_mix, norm_gain, w_gate, w_up):
    mesh_sizes = (lax.axis_size("seq"), lax.axis_size("dp"))
    if mesh_sizes == (SEQ_COUNT, DP_COUNT) and x_in.shape[1] == SPAN:
        local = (x_in, gate_in, keys_b, queries_c, decay_log, level_mix)
        layer = streamed_layer(*(array[0] for array in local), norm_gain, w_gate, w_up)
        return layer[None]
    tok_dev = x_in.shape[1]
    embedding_width = x_in.shape[2]
    head_count = decay_log.shape[1]
    head_dim = embedding_width // head_count
    blocks = tok_dev // SPAN
    inner_count = SPAN_BITS + 1
    seq_bits = lax.axis_size("seq").bit_length() - 1
    x_blocks = x_in[0].reshape(blocks, SPAN, head_count, head_dim)
    b_blocks = keys_b[0].reshape(blocks, SPAN, -1)
    c_blocks = queries_c[0].reshape(blocks, SPAN, -1)
    a_blocks = decay_log[0].reshape(head_count, blocks, SPAN)
    mix_all = level_mix[0].reshape(level_mix.shape[1], head_count, blocks, SPAN)
    local_parts, block_states, block_decays, runnings = ([], [], [], [])
    block_index = 0
    local_part, block_state, running = block_inner(
        x_blocks[block_index],
        b_blocks[block_index],
        c_blocks[block_index],
        a_blocks[:, block_index],
        mix_all[:inner_count, :, block_index],
    )
    local_parts.append(local_part)
    block_states.append(block_state)
    block_decays.append(running[:, -1])
    runnings.append(running)
    summary = jnp.zeros_like(block_states[0])
    block_index = 0
    summary = (
        jnp.exp(block_decays[block_index])[:, None, None] * summary + block_states[block_index]
    )
    summary_decay = block_decays[block_index]
    rank_here = lax.axis_index("seq")
    own_prefix = jnp.zeros((head_count,), jnp.float32)
    device_levels = []
    for bit_index in range(seq_bits):
        other_state, other_decay = swapped((summary.astype(jnp.bfloat16), summary_decay), "seq", bit_index)
        other_state = other_state.astype(jnp.float32)
        is_upper = rank_here >> bit_index & 1 == 1
        device_levels.append(
            jnp.where(is_upper, jnp.exp(own_prefix)[:, None, None] * other_state, 0.0)
        )
        lower_state = jnp.where(is_upper, other_state, summary)
        lower_decay = jnp.where(is_upper, other_decay, summary_decay)
        upper_state = jnp.where(is_upper, summary, other_state)
        upper_decay = jnp.where(is_upper, summary_decay, other_decay)
        summary = jnp.exp(upper_decay)[:, None, None] * lower_state + upper_state
        summary_decay = lower_decay + upper_decay
        own_prefix = jnp.where(is_upper, own_prefix + other_decay, own_prefix)
    zero_decay = jnp.zeros((head_count,), jnp.float32)
    block_index = 0
    levels = []
    lead_decay = sum(block_decays[:block_index], zero_decay)
    for device_level in device_levels:
        levels.append(jnp.exp(lead_decay)[:, None, None] * device_level)
    distant = block_distant(
        c_blocks[block_index], runnings[block_index], mix_all[inner_count:, :, block_index], levels
    )
    outputs = local_parts[block_index] + distant
    mixed = outputs.reshape(tok_dev, embedding_width)
    gated = mixed * jax.nn.silu(gate_in[0].astype(jnp.float32))
    normed = (
        gated * lax.rsqrt(jnp.mean(gated * gated, axis=-1, keepdims=True) + EPS) * norm_gain
    ).astype(jnp.bfloat16)
    return gathered_projection(normed, w_gate, w_up)[None]


def solution(mesh):
    in_specs = (
        P("dp", "seq", None),
        P("dp", "seq", None),
        P("dp", "seq", None),
        P("dp", "seq", None),
        P("dp", None, "seq"),
        P("dp", None, None, "seq"),
        P(),
        P(None, ("seq", "dp")),
        P(None, ("seq", "dp")),
    )
    out_specs = P("dp", "seq", None)
    return jax.shard_map(
        per_device, mesh=mesh, in_specs=in_specs, out_specs=out_specs, check_vma=False
    )
```

```python
import jax
import jax.numpy as jnp
from jax import lax
from jax.experimental import pallas as pl
from jax.experimental.pallas import tpu as pltpu
from jax.sharding import PartitionSpec as P

SPAN = 256
SPAN_BITS = 8


EPS = 1e-05
HIGH = lax.Precision.HIGHEST


def swapped(value, axis, distance):
    mask = 2**distance
    pairs = [(source, source ^ mask) for source in range(lax.axis_size(axis))]
    return lax.ppermute(value, axis, pairs)


def top_bit(values):
    powers = jnp.arange(1, 31, dtype=jnp.int32)
    return jnp.sum(values[..., None] >> powers > 0, axis=-1)


def block_inner(x_blk, b_blk, c_blk, a_blk, mix_low):
    length = a_blk.shape[1]
    inner_count = mix_low.shape[0]
    running = jnp.cumsum(a_blk, axis=1)
    position = jnp.arange(length, dtype=jnp.int32)
    differ = position[:, None] ^ position[None, :]
    level_table = jnp.where(differ > 0, top_bit(differ) + 1, 0)
    level_picks = (
        level_table[None] == jnp.arange(inner_count, dtype=jnp.int32)[:, None, None]
    ).astype(jnp.float32)
    chosen = jnp.einsum("lht,lts->hts", mix_low, level_picks, precision=HIGH)
    causal_mask = position[:, None] >= position[None, :]
    log_gap = jnp.where(causal_mask[None], running[:, :, None] - running[:, None, :], -jnp.inf)
    scores = jnp.dot(c_blk, b_blk.T, preferred_element_type=jnp.float32)
    weights = (chosen * jnp.exp(log_gap) * scores[None]).astype(jnp.bfloat16)
    local_part = jnp.einsum("hts,shp->thp", weights, x_blk, preferred_element_type=jnp.float32)
    tail_decay = jnp.exp(running[:, -1:] - running)
    scaled_keys = (tail_decay.T[:, :, None] * b_blk[:, None, :]).astype(jnp.bfloat16)
    block_state = jnp.einsum("shn,shp->hnp", scaled_keys, x_blk, preferred_element_type=jnp.float32)
    return (local_part, block_state, running)


def block_distant(c_blk, running, mix_high, levels):
    growth = jnp.exp(running)
    distant_sum = jnp.zeros((c_blk.shape[0], running.shape[0], levels[0].shape[2]), jnp.float32)
    for level_rank in range(len(levels)):
        level_scale = (mix_high[level_rank] * growth).T
        product = jnp.einsum(
            "tn,hnp->thp",
            c_blk,
            levels[level_rank].astype(jnp.bfloat16),
            preferred_element_type=jnp.float32,
        )
        distant_sum = distant_sum + level_scale[:, :, None] * product
    return distant_sum


def gathered_projection(normed, w_gate, w_up):
    tok_dev = normed.shape[0]
    paired = jnp.stack([w_gate, w_up])
    dp_count = lax.axis_size("dp")
    seq_count = lax.axis_size("seq")
    seq_weights = lax.all_gather(paired, "seq", axis=2, tiled=True)
    projected = jnp.einsum(
        "td,gdk->gtk",
        normed,
        lax.all_gather(seq_weights, "dp", axis=2, tiled=True),
        preferred_element_type=jnp.float32,
    )
    returned = (jax.nn.silu(projected[0]) * projected[1]).astype(jnp.bfloat16)
    hidden = (
        returned.reshape(tok_dev, dp_count, seq_count, -1)
        .transpose(0, 2, 1, 3)
        .reshape(tok_dev, -1)
    )
    return hidden


MESH = pl.DeviceIdType.MESH
SEQ_COUNT = 8
DP_COUNT = 4
LINE = 4
CHIPS = 16


def line_member(z, steps):
    place = z + (z >= 2) * (5 - 2 * z)
    back = lax.rem(place - steps + 2 * LINE, LINE)
    return back + (back >= 2) * (5 - 2 * back)


class Gather:
    def __init__(self, piece, held, z_sems, x_sems, y_sems, core_sems, own_sem):
        self.piece, self.held, self.own_sem = piece, held, own_sem
        self.sems = {"z": z_sems, "x": x_sems, "y": y_sems, "core": core_sems}
        seq, dp = lax.axis_index("seq"), lax.axis_index("dp")
        self.seq, self.dp = seq, dp
        self.z, self.x, self.y, self.core = seq // 2, lax.rem(seq, 2), dp // 2, lax.rem(dp, 2)
        self.targets = {
            "z": (line_member(self.z, -1) * 2 + self.x, dp),
            "x": (self.z * 2 + 1 - self.x, dp),
            "y": (seq, (1 - self.y) * 2 + self.core),
            "core": (seq, self.y * 2 + 1 - self.core),
        }
        self.before = (line_member(self.z, 1) * 2 + self.x, dp)
        rows = piece.shape[0]
        cut = (rows // 2 + 15) // 16 * 16
        self.cuts = ((0, cut), (cut, rows - cut))
        self.sent = []

    def greet(self):
        barrier = pltpu.get_barrier_semaphore()
        others = list(self.targets.values()) + [self.before]
        for other in others:
            pl.semaphore_signal(barrier, inc=1, device_id=other, device_id_type=MESH)
        pl.semaphore_wait(barrier, len(others))

    def chip(self, step, flip_x, flip_y):
        x = 1 - self.x if flip_x else self.x
        y = 1 - self.y if flip_y else self.y
        return line_member(self.z, step) * 4 + x * 2 + y

    def copy(self, way, slot, chip, part, own=False):
        first, count = self.cuts[part]
        place = self.held.at[chip, self.core, pl.ds(first, count)]
        return pltpu.make_async_remote_copy(
            src_ref=self.piece.at[pl.ds(first, count)] if own else place,
            dst_ref=place,
            send_sem=self.sems[way].at[0, slot],
            recv_sem=self.sems[way].at[1, slot],
            device_id=self.targets[way],
            device_id_type=MESH,
        )

    def send(self, way, slot, chip, part, own=False):
        copy = self.copy(way, slot, chip, part, own)
        copy.start()
        self.sent.append(copy)

    def start(self):
        chip = self.chip(0, 0, 0)
        self.own = pltpu.make_async_copy(self.piece, self.held.at[chip, self.core], self.own_sem)
        self.own.start()
        for way in ("z", "x", "y", "core"):
            for part in range(2):
                self.send(way, part, chip, part, own=True)

    def line(self, step, part):
        chip = self.chip(step, 0, 0)
        self.copy("z", (step - 1) * 2 + part, chip, part).wait_recv()
        if step < LINE - 1:
            self.send("z", step * 2 + part, chip, part)
        for way in ("x", "y"):
            self.send(way, step * 2 + part, chip, part)
        self.send("core", step * 8 + part, chip, part)

    def across_x(self, step, part):
        chip = self.chip(step, 1, 0)
        self.copy("x", step * 2 + part, chip, part).wait_recv()
        if part == 0:
            self.send("y", 2 * LINE + step, chip, part)
        self.send("core", step * 8 + 2 + part, chip, part)

    def across_y(self, step, part):
        chip = self.chip(step, 0, 1)
        self.copy("y", step * 2 + part, chip, part).wait_recv()
        if part == 1:
            self.send("x", 2 * LINE + step, chip, part)
        self.send("core", step * 8 + 4 + part, chip, part)

    def across(self, step, part):
        self.across_x(step, part)
        self.across_y(step, part)

    def corner(self, step):
        chip = self.chip(step, 1, 1)
        for part, way in enumerate(("y", "x")):
            self.copy(way, 2 * LINE + step, chip, part).wait_recv()
            self.send("core", step * 8 + 6 + part, chip, part)

    def ready(self, step, kind):
        chip = self.chip(step, kind % 2, kind // 2)
        for part in range(2):
            first, count = self.cuts[part]
            place = self.held.at[chip, 1 - self.core, pl.ds(first, count)]
            slot = step * 8 + kind * 2 + part
            pltpu.make_async_remote_copy(
                src_ref=place,
                dst_ref=place,
                send_sem=self.sems["core"].at[0, slot],
                recv_sem=self.sems["core"].at[1, slot],
                device_id=self.targets["core"],
                device_id_type=MESH,
            ).wait_recv()
        return chip

    def finish(self):
        for copy in self.sent:
            copy.wait_send()


NT = (((1,), (1,)), ((), ()))
HALF = SPAN // 2
GROUP = 4


def rows_of(index, count):
    return pl.ds(pl.multiple_of(index * count, count), count)


def layer_kernel(
    x_in, gate_in, keys, queries, decay, mix, gain, piece, hidden,
    held, x_cols, gate_cols, gain_cols, normed, mixed, run_col, run_row, tail, level_scale,
    level_of, scores, state, state_out, state_in, decay_out, decay_in,
    z_sems, x_sems, y_sems, core_sems, own_sem, state_sems, decay_sems,
):
    gather = Gather(piece, held, z_sems, x_sems, y_sems, core_sems, own_sem)
    gather.greet()
    gather.start()
    heads = decay.shape[0]
    head_dim = x_cols.shape[0] // heads
    seq, dp = gather.seq, gather.dp
    f32, bf16 = jnp.float32, jnp.bfloat16

    def exchange(bit):
        target = (seq + (1 - 2 * (seq // 2**bit % 2)) * 2**bit, dp)
        pairs = [(state_out, state_in, state_sems), (decay_out, decay_in, decay_sems)]
        return [
            pltpu.make_async_remote_copy(
                src_ref=source.at[bit],
                dst_ref=place.at[bit],
                send_sem=sems.at[0, bit],
                recv_sem=sems.at[1, bit],
                device_id=target,
                device_id_type=MESH,
            )
            for source, place, sems in pairs[: 1 if bit == 2 else 2]
        ]

    before = lax.broadcasted_iota(jnp.int32, (SPAN, SPAN), 0)
    after = lax.broadcasted_iota(jnp.int32, (SPAN, SPAN), 1)
    up_to = (before <= after).astype(f32)
    run = jnp.dot(decay[...], up_to, precision=HIGH, preferred_element_type=f32)
    run_row[...] = run
    tail[...] = jnp.exp(jnp.minimum(run[:, SPAN - 1 :] - run, 0.0))
    total = jnp.broadcast_to(run[:, SPAN - 1 :], (heads, 128))
    decay_out[0] = total

    def turn(index, _):
        lanes = rows_of(index, 128)
        x_cols[lanes, :] = x_in[:, lanes].astype(f32).T.astype(bf16)
        return 0

    lax.fori_loop(0, x_cols.shape[0] // 128, turn, 0)

    def block_states(index, _):
        parts = []
        for place in range(GROUP):
            head = index * GROUP + place
            values = x_cols[rows_of(head, head_dim), :].astype(f32) * tail[pl.ds(head, 1), :]
            parts.append(values.astype(bf16))
        rows = rows_of(index, GROUP * head_dim)
        result = jnp.dot(jnp.concatenate(parts), keys[...], preferred_element_type=f32)
        state[rows, :] = result
        state_out[0, rows, :] = result.astype(bf16)
        return 0

    lax.fori_loop(0, heads // GROUP, block_states, 0)
    rounds = [exchange(0)]
    for copy in rounds[0]:
        copy.start()

    gather.line(1, 0)
    gather.across(0, 0)

    columns = lax.dot_general(
        (before >= after).astype(f32), decay[...], NT, precision=HIGH, preferred_element_type=f32
    )
    for head in range(heads):
        run_col[head] = jnp.broadcast_to(columns[:, head : head + 1], (SPAN, 128))
    scores[...] = lax.dot_general(keys[...], queries[...], NT, preferred_element_type=f32)
    source = lax.broadcasted_iota(jnp.int32, (HALF, HALF), 0)
    target = lax.broadcasted_iota(jnp.int32, (HALF, HALF), 1)
    differ = source ^ target
    level = jnp.zeros((HALF, HALF), jnp.int32)
    for bit in range(SPAN_BITS - 1):
        level = level + (differ >= 2**bit).astype(jnp.int32)
    level_of[...] = jnp.where(source <= target, level, -1)

    gather.line(1, 1)
    gather.across(0, 1)

    def local(head, _):
        run_t = run_row[pl.ds(head, 1), :]
        mixes = [mix[rank, pl.ds(head, 1), :] for rank in range(SPAN_BITS + 1)]
        values = x_cols[rows_of(head, head_dim), :]
        weights = []
        for first in (0, HALF):
            span = slice(first, first + HALF)
            gap = run_t[:, span] - run_col[head, span, :]
            levels = level_of[...]
            chosen = jnp.zeros((HALF, HALF), f32)
            for rank in range(SPAN_BITS):
                chosen = jnp.where(levels == rank, mixes[rank][:, span], chosen)
            weights.append(chosen * jnp.exp(jnp.minimum(gap, 0.0)) * scores[span, span])
        gap = run_t[:, HALF:] - run_col[head, :HALF, :]
        cross = mixes[SPAN_BITS][:, HALF:] * jnp.exp(jnp.minimum(gap, 0.0))
        cross = (cross * scores[:HALF, HALF:]).astype(bf16)
        rows = rows_of(head, head_dim)
        mixed[rows, :HALF] = jnp.dot(
            values[:, :HALF], weights[0].astype(bf16), preferred_element_type=f32
        )
        mixed[rows, HALF:] = jnp.dot(
            values, jnp.concatenate([cross, weights[1].astype(bf16)]), preferred_element_type=f32
        )
        return 0

    def locals_of(quarter):
        lax.fori_loop(quarter * heads // 4, (quarter + 1) * heads // 4, local, 0)

    prefix = jnp.zeros((heads, 128), f32)

    def scale_level(bit, prefix):
        upper = (seq // 2**bit % 2).astype(f32)
        growth = jnp.exp(run_row[...] + jnp.concatenate([prefix] * 2, axis=1))
        level_scale[bit] = upper * mix[SPAN_BITS + 1 + bit] * growth

    def merge(bit, total, prefix):
        for copy in rounds[bit]:
            copy.wait_recv()
        other = decay_in[bit]
        upper = (seq // 2**bit % 2).astype(f32)
        scale_level(bit, prefix)
        tail[:, :128] = jnp.exp((1.0 - upper) * other)
        tail[:, 128:] = jnp.exp(upper * total)

        def add(head, _):
            rows = rows_of(head, head_dim)
            factors = tail[pl.ds(head, 1), :]
            mine = factors[:, :128] * state[rows, :]
            both = mine + factors[:, 128:] * state_in[bit, rows, :].astype(f32)
            state[rows, :] = both
            state_out[bit + 1, rows, :] = both.astype(bf16)
            return 0

        lax.fori_loop(0, heads, add, 0)
        total = total + other
        if bit == 0:
            decay_out[1] = total
        rounds.append(exchange(bit + 1))
        for copy in rounds[bit + 1]:
            copy.start()
        return total, prefix + upper * other

    def distant(bit):
        def add(index, _):
            rows = rows_of(index, GROUP * head_dim)
            product = lax.dot_general(
                state_in[bit, rows, :], queries[...], NT, preferred_element_type=f32
            )
            for place in range(GROUP):
                head = index * GROUP + place
                part = product[place * head_dim : (place + 1) * head_dim]
                mixed[rows_of(head, head_dim), :] += level_scale[bit, pl.ds(head, 1), :] * part
            return 0

        lax.fori_loop(0, heads // GROUP, add, 0)

    locals_of(0)
    gather.line(2, 0)
    total, prefix = merge(0, total, prefix)
    gather.across(1, 0)
    locals_of(1)
    gather.line(2, 1)
    gather.across(1, 1)
    locals_of(2)
    gather.line(3, 0)
    gather.corner(0)
    total, prefix = merge(1, total, prefix)
    scale_level(2, prefix)
    gather.line(3, 1)
    gather.across(2, 0)
    locals_of(3)
    gather.corner(1)
    gather.across(2, 1)
    distant(0)
    distant(1)

    def turn_gate(index, _):
        lanes = rows_of(index, 128)
        gate_cols[lanes, :] = gate_in[:, lanes].astype(f32).T.astype(bf16)
        gain_cols[lanes, :] = jnp.broadcast_to(gain[:, lanes], (128, 128)).T
        return 0

    lax.fori_loop(0, gate_cols.shape[0] // 128, turn_gate, 0)
    gather.across(3, 0)
    gather.across(3, 1)
    rounds[2][0].wait_recv()
    distant(2)

    def gated(index, squares):
        rows = rows_of(index, head_dim)
        gate = gate_cols[rows, :].astype(f32)
        value = mixed[rows, :] * (gate / (1.0 + jnp.exp(-gate)))
        mixed[rows, :] = value
        return squares + jnp.sum(value * value, axis=0, keepdims=True)

    squares = lax.fori_loop(0, heads, gated, jnp.zeros((1, SPAN), f32))
    scale = lax.rsqrt(squares / mixed.shape[0] + EPS)

    def norm(index, _):
        rows = rows_of(index, head_dim)
        gains = gain_cols[rows, :]
        value = mixed[rows, :] * scale * jnp.concatenate([gains, gains], axis=1)
        normed[rows, :] = value.astype(bf16)
        return 0

    lax.fori_loop(0, heads, norm, 0)

    rows = piece.shape[0]

    def project_pair(step, kind):
        chip = gather.ready(step, kind) // 2 * 2
        gather.ready(step, kind + 2)
        weights = held[pl.ds(chip, 2)].reshape(4 * rows, held.shape[3])
        both = jnp.dot(weights, normed[...], preferred_element_type=f32)
        both = both.reshape(2, 2, rows, SPAN)
        gate, up = both[:, 0], both[:, 1]
        hidden[pl.ds(chip, 2)] = (gate / (1.0 + jnp.exp(-gate)) * up).astype(bf16)

    gather.own.wait()
    for step in range(2):
        project_pair(step, 0)
        project_pair(step, 1)
    gather.corner(2)
    project_pair(2, 0)
    project_pair(2, 1)
    project_pair(3, 0)
    gather.corner(3)
    project_pair(3, 1)
    gather.finish()
    for copies in rounds:
        for copy in copies:
            copy.wait_send()


def chip_rows(w_gate, w_up):
    first = lax.axis_index("dp") % 2 == 0
    gate, up = w_gate.T, w_up.T
    pairs = [(source, source ^ 1) for source in range(DP_COUNT)]
    other = lax.ppermute(jnp.where(first, up, gate), "dp", pairs)
    return jnp.where(first, jnp.concatenate([gate, other]), jnp.concatenate([other, up]))


def streamed_layer(x, gate, keys, queries, decay, mix, norm_gain, w_gate, w_up):
    piece = chip_rows(w_gate, w_up)
    rows, depth = piece.shape
    tokens = x.shape[0]
    heads = decay.shape[0]
    states = keys.shape[1]
    sems = pltpu.SemaphoreType.DMA
    f32, bf16 = jnp.float32, jnp.bfloat16
    hidden = pl.pallas_call(
        layer_kernel,
        out_shape=jax.ShapeDtypeStruct((CHIPS, rows, tokens), bf16),
        in_specs=[pl.BlockSpec(memory_space=pltpu.VMEM)] * 8,
        out_specs=pl.BlockSpec(memory_space=pltpu.VMEM),
        scratch_shapes=[
            pltpu.VMEM((CHIPS, 2, rows, depth), bf16),
            pltpu.VMEM((depth, tokens), bf16),
            pltpu.VMEM((depth, tokens), bf16),
            pltpu.VMEM((depth, 128), f32),
            pltpu.VMEM((depth, tokens), bf16),
            pltpu.VMEM((depth, tokens), f32),
            pltpu.VMEM((heads, tokens, 128), f32),
            pltpu.VMEM((heads, tokens), f32),
            pltpu.VMEM((heads, tokens), f32),
            pltpu.VMEM((3, heads, tokens), f32),
            pltpu.VMEM((HALF, HALF), jnp.int32),
            pltpu.VMEM((SPAN, SPAN), f32),
            pltpu.VMEM((depth, states), f32),
            pltpu.VMEM((3, depth, states), bf16),
            pltpu.VMEM((3, depth, states), bf16),
            pltpu.VMEM((2, heads, 128), f32),
            pltpu.VMEM((2, heads, 128), f32),
            sems((2, 6)),
            sems((2, 12)),
            sems((2, 12)),
            sems((2, 2 * CHIPS)),
            sems,
            sems((2, 3)),
            sems((2, 2)),
        ],
        compiler_params=pltpu.CompilerParams(
            collective_id=0, has_side_effects=True, vmem_limit_bytes=56 * 2**20
        ),
        cost_estimate=pl.CostEstimate(
            flops=4 * tokens * CHIPS * rows * depth,
            bytes_accessed=2 * CHIPS * rows * depth * 2,
            transcendentals=tokens * CHIPS * rows,
        ),
    )(x, gate, keys, queries, decay, mix, norm_gain[None, :], piece)
    return hidden.reshape(CHIPS * rows, tokens).T


def per_device(x_in, gate_in, keys_b, queries_c, decay_log, level_mix, norm_gain, w_gate, w_up):
    mesh_sizes = (lax.axis_size("seq"), lax.axis_size("dp"))
    if mesh_sizes == (SEQ_COUNT, DP_COUNT) and x_in.shape[1] == SPAN:
        local = (x_in, gate_in, keys_b, queries_c, decay_log, level_mix)
        layer = streamed_layer(*(array[0] for array in local), norm_gain, w_gate, w_up)
        return layer[None]
    tok_dev = x_in.shape[1]
    embedding_width = x_in.shape[2]
    head_count = decay_log.shape[1]
    head_dim = embedding_width // head_count
    blocks = tok_dev // SPAN
    inner_count = SPAN_BITS + 1
    seq_bits = lax.axis_size("seq").bit_length() - 1
    x_blocks = x_in[0].reshape(blocks, SPAN, head_count, head_dim)
    b_blocks = keys_b[0].reshape(blocks, SPAN, -1)
    c_blocks = queries_c[0].reshape(blocks, SPAN, -1)
    a_blocks = decay_log[0].reshape(head_count, blocks, SPAN)
    mix_all = level_mix[0].reshape(level_mix.shape[1], head_count, blocks, SPAN)
    local_parts, block_states, block_decays, runnings = ([], [], [], [])
    block_index = 0
    local_part, block_state, running = block_inner(
        x_blocks[block_index],
        b_blocks[block_index],
        c_blocks[block_index],
        a_blocks[:, block_index],
        mix_all[:inner_count, :, block_index],
    )
    local_parts.append(local_part)
    block_states.append(block_state)
    block_decays.append(running[:, -1])
    runnings.append(running)
    summary = jnp.zeros_like(block_states[0])
    block_index = 0
    summary = (
        jnp.exp(block_decays[block_index])[:, None, None] * summary + block_states[block_index]
    )
    summary_decay = block_decays[block_index]
    rank_here = lax.axis_index("seq")
    own_prefix = jnp.zeros((head_count,), jnp.float32)
    device_levels = []
    for bit_index in range(seq_bits):
        other_state, other_decay = swapped((summary.astype(jnp.bfloat16), summary_decay), "seq", bit_index)
        other_state = other_state.astype(jnp.float32)
        is_upper = rank_here >> bit_index & 1 == 1
        device_levels.append(
            jnp.where(is_upper, jnp.exp(own_prefix)[:, None, None] * other_state, 0.0)
        )
        lower_state = jnp.where(is_upper, other_state, summary)
        lower_decay = jnp.where(is_upper, other_decay, summary_decay)
        upper_state = jnp.where(is_upper, summary, other_state)
        upper_decay = jnp.where(is_upper, summary_decay, other_decay)
        summary = jnp.exp(upper_decay)[:, None, None] * lower_state + upper_state
        summary_decay = lower_decay + upper_decay
        own_prefix = jnp.where(is_upper, own_prefix + other_decay, own_prefix)
    zero_decay = jnp.zeros((head_count,), jnp.float32)
    block_index = 0
    levels = []
    lead_decay = sum(block_decays[:block_index], zero_decay)
    for device_level in device_levels:
        levels.append(jnp.exp(lead_decay)[:, None, None] * device_level)
    distant = block_distant(
        c_blocks[block_index], runnings[block_index], mix_all[inner_count:, :, block_index], levels
    )
    outputs = local_parts[block_index] + distant
    mixed = outputs.reshape(tok_dev, embedding_width)
    gated = mixed * jax.nn.silu(gate_in[0].astype(jnp.float32))
    normed = (
        gated * lax.rsqrt(jnp.mean(gated * gated, axis=-1, keepdims=True) + EPS) * norm_gain
    ).astype(jnp.bfloat16)
    return gathered_projection(normed, w_gate, w_up)[None]


def solution(mesh):
    in_specs = (
        P("dp", "seq", None),
        P("dp", "seq", None),
        P("dp", "seq", None),
        P("dp", "seq", None),
        P("dp", None, "seq"),
        P("dp", None, None, "seq"),
        P(),
        P(None, ("seq", "dp")),
        P(None, ("seq", "dp")),
    )
    out_specs = P("dp", "seq", None)
    return jax.shard_map(
        per_device, mesh=mesh, in_specs=in_specs, out_specs=out_specs, check_vma=False
    )
```
